768 devices in a mesh: wide: 12 (over z_lo, core), narrow: 64 (over x, z_hi, y).
Axes of the slice: x: 4, y: 8, z: 12 (z_hi: 2, z_lo: 6; z = z_hi * 6 + z_lo), core: 2. Of those that a mesh axis runs over, the one named last changes fastest.
Arguments:
- grad_parts: bfloat16 [12, 3584, 8192], P('wide', 'narrow'), may hold values from -6 to 6
- master: bfloat16 [3584, 8192], P('narrow'), may hold values from -0.1875 to 0.1875
- moment_one: float32 [3584, 8192], P('narrow'), may hold values from -4 to 4
- moment_two: float32 [3584, 8192], P('narrow'), may hold values from 0.01 to 1
- gate_up: bfloat16 [3584, 2, 8192], P(None, None, 'narrow'), may hold values from -0.09375 to 0.09375
- tokens: bfloat16 [1536, 3584], P(('wide', 'narrow')), may hold values from -6 to 6
- expert_ids: int32 [1536, 4], P(('wide', 'narrow')), may hold values from 0 to 7, all different within a row; in each aligned block of 2 rows (0 to 1, 2 to 3, ...) at most 2 rows name the same one
- gate_vals: bfloat16 [1536, 4], P(('wide', 'narrow')), may hold values from 0.049804688 to 1
Outputs:
- new_master: bfloat16 [3584, 8192], P('narrow')
- new_one: float32 [3584, 8192], P('narrow')
- new_two: float32 [3584, 8192], P('narrow')
- combined: bfloat16 [1536, 3584], P(('wide', 'narrow'))
The draws below stay inside these ranges and needn't reach their ends.
Inputs may be any that keep to these rules, and one draw needn't show every extreme that they name: `expert_ids`: each token names 4 distinct experts; each device's 2 tokens name every expert at most 2 times (which follows from the distinct ids), and some device names one expert twice.
All inputs are finite; a program needn't handle non-finite values.
Results may differ from the reference program's by a relative error of at most 0.022.
Values may be sent and summed in bfloat16 or wider, within the bound.
A program may use at most 64 MiB of HBM per device.

```python
import math
import jax
import jax.numpy as jnp
import numpy as np
from jax import lax

D = 3584
FF = 1024
EXPERTS = 8
TOPK = 4
QBLOCK = 128
TOK_DEV = 2
CAP = 2
TOKENS = 1536
N_WIDE = 12
N_NARROW = 64


def steps_of(own_key, shape, shards, smallest, top_value):
    def one(position, shards_of):
        heights = jax.random.uniform(jax.random.fold_in(jax.random.fold_in(own_key, 6), position), (shards_of,), jnp.float32, smallest / len(shards), top_value / len(shards))
        return jnp.repeat(jnp.exp(heights), shape[position] // shards_of).reshape((-1,) + (1,) * (len(shape) - position - 1))

    gain = one(*shards[0])
    for cut in shards[1:]:
        gain = gain * one(*cut)
    return gain


def assign_block(own_key, own, number, rows, count, top, reach, slope):
    sequence = jax.random.permutation(own_key, count)
    heavy_load, common = shares(count, rows * top, reach, slope, True), shares(count, rows * top, reach, slope, False)
    places = jnp.arange(count)

    def named(sizes, turn):
        used = int((sizes > 0).sum())
        fixed = max(1, used // 4)
        moved = fixed + (places - fixed + turn * (used - fixed)) % max(1, count - fixed)
        return jnp.zeros((count,), jnp.int32).at[sequence[jnp.where(places < fixed, places, moved)]].set(jnp.asarray(sizes, jnp.int32))

    sizes = jnp.where(number % 4 == 0, named(heavy_load, number // 4), named(common, number - number // 4 - 1))
    mixed = jax.random.permutation(jax.random.fold_in(own, 3), count)
    source_of, receiver = mixed[0:count // 2 * 2:2], mixed[1:count // 2 * 2:2]
    slack = jnp.minimum(sizes[source_of] - 1, reach - sizes[receiver]) // 2
    slack = jnp.where((source_of == sequence[0]) | (receiver == sequence[0]) | (sizes[receiver] == 0), 0, jnp.maximum(slack, 0))
    moved = jax.random.randint(jax.random.fold_in(own, 4), (count // 2,), 0, 1 << 20) % (slack + 1)
    sizes = sizes.at[source_of].add(-moved).at[receiver].add(moved)
    members = jnp.searchsorted(jnp.cumsum(sizes), jnp.arange(rows * top), side="right").astype(jnp.int32)
    listing = members.reshape(top, rows).T
    listing = listing[jax.random.permutation(jax.random.fold_in(own, 1), rows)]
    turn = jax.random.randint(jax.random.fold_in(own, 2), (rows, 1), 0, top)
    return jnp.take_along_axis(listing, (jnp.arange(top)[None, :] + turn) % top, axis=1)


def shares(count, total, limit, lean, full):
    loads = [(1 << 20) // math.isqrt(grade ** lean) + 1 for grade in range(1, count + 1)]
    largest = limit if full else min(limit, max(-(-total // count), total * loads[0] // sum(loads)))
    least = 1 if total - largest >= count - 1 else 0
    counts, surplus = [largest] + [least] * (count - 1), total - largest - least * (count - 1)
    while surplus > 0:
        free = [i for i in range(1, count) if counts[i] < largest] or [i for i in range(1, count) if counts[i] < limit]
        pool, remaining = sum([loads[i] for i in free]), surplus
        for i in free:
            addition = min(limit - counts[i], max(1, remaining * loads[i] // pool), surplus)
            counts[i] = counts[i] + addition
            surplus = surplus - addition
    return np.array(counts)


def gaussian(rng, extent, deviation, reach, split=(), held_as=jnp.bfloat16):
    entries = jax.random.normal(rng, extent, jnp.float32) * deviation
    if len(split) > 0:
        entries = steps_of(rng, extent, split, -0.22, 0.18) * entries
    return jnp.clip(entries, min=-reach, max=reach).astype(held_as)


def setup_inputs(seed: int = 0) -> dict:
    splits = jax.random.split(jax.random.key(seed), 9)
    grad_parts = gaussian(splits[0], (N_WIDE, D, EXPERTS * FF), 1.0, 6.0, ((0, 12), (1, 64)))
    master = gaussian(splits[1], (D, EXPERTS * FF), FF ** -0.5, 0.1875, ((0, 64),))
    moment_one = gaussian(splits[2], (D, EXPERTS * FF), 0.3, 4.0, ((0, 64),), jnp.float32)
    moment_two = jnp.clip(jnp.exp(math.log(1.0) - 4.6051702 * jax.random.uniform(splits[3], (D, EXPERTS * FF), jnp.float32) ** steps_of(splits[3], (D, EXPERTS * FF), ((0, 64),), -0.2, 0.2)), 0.01, 1.0)
    gate_up = gaussian(splits[4], (D, 2, EXPERTS * FF), D ** -0.5, 0.09375, ((2, 64),))
    tokens = gaussian(splits[5], (TOKENS, D), 1.0, 6.0, ((0, 768),))
    expert_ids_keys = jax.random.split(jax.random.fold_in(splits[6], 1), TOKENS // TOK_DEV)
    expert_ids_turns = jax.random.permutation(jax.random.fold_in(splits[6], 3), TOKENS // TOK_DEV)
    expert_ids = jax.vmap(lambda own, number: assign_block(jax.random.fold_in(splits[6], 2), own, number, TOK_DEV, EXPERTS, TOPK, CAP, 2))(expert_ids_keys, expert_ids_turns).reshape((TOKENS, TOPK))
    gate_vals = jnp.clip(0.049804688 + 0.9501953 * jax.random.uniform(splits[7], (TOKENS, TOPK), jnp.float32) ** steps_of(splits[7], (TOKENS, TOPK), ((0, 768),), -0.2, 0.2), 0.049804688, 1.0).astype(jnp.bfloat16)
    return {"grad_parts": grad_parts, "master": master, "moment_one": moment_one, "moment_two": moment_two, "gate_up": gate_up, "tokens": tokens, "expert_ids": expert_ids, "gate_vals": gate_vals}


beta_first = 0.9
beta_second = 0.95
learn_rate = 0.003
adam_eps = 1e-08
quant_limit = 448.0
amax_eps = 1e-06
bias_first = 1.0 - 0.9 ** 10
bias_second = 1.0 - 0.95 ** 10

def adam_quant(grad_sum, master, moment_one, moment_two):
    new_one = beta_first * moment_one + (1.0 - beta_first) * grad_sum
    new_two = beta_second * moment_two + (1.0 - beta_second) * grad_sum * grad_sum
    step_dir = new_one / bias_first / (jnp.sqrt(new_two / bias_second) + adam_eps)
    updated = master.astype(jnp.float32) - learn_rate * step_dir
    row_count, col_count = updated.shape
    blocks = updated.reshape(row_count, col_count // QBLOCK, QBLOCK)
    scales = ((lax.optimization_barrier(jnp.max(jnp.abs(blocks), axis=2)) + amax_eps) / quant_limit).astype(jnp.bfloat16)
    quanta = (blocks / scales.astype(jnp.float32)[:, :, None]).astype(jnp.bfloat16).reshape(row_count, col_count)
    return (updated.astype(jnp.bfloat16), new_one, new_two, quanta, scales)

def expert_rows(rows_in, gate_piece, quanta, scales):
    unit_count = gate_piece.shape[2]
    proj_both = jnp.dot(rows_in, gate_piece.reshape(gate_piece.shape[0], 2 * unit_count), preferred_element_type=jnp.float32)
    hidden = (jax.nn.silu(proj_both[:, :unit_count]) * proj_both[:, unit_count:]).astype(jnp.bfloat16)
    block_count = unit_count // QBLOCK
    per_block = jnp.einsum('rbf,dbf->rbd', hidden.reshape(-1, block_count, QBLOCK).astype(jnp.float32), quanta.reshape(quanta.shape[0], block_count, QBLOCK).astype(jnp.float32))
    return jnp.einsum('rbd,db->rd', per_block, scales.astype(jnp.float32))

def reference(grad_parts, master, moment_one, moment_two, gate_up, tokens, expert_ids, gate_vals):
    grad_sum = jnp.zeros(master.shape, jnp.float32)
    for replica in range(N_WIDE):
        grad_sum = grad_sum + grad_parts[replica].astype(jnp.float32)
    new_master, new_one, new_two, quanta, scales = adam_quant(grad_sum, master, moment_one, moment_two)
    onehot = (expert_ids[:, :, None] == jnp.arange(EXPERTS, dtype=jnp.int32)[None, None, :]).astype(jnp.float32)
    weights_tok = lax.optimization_barrier(jnp.sum(onehot * gate_vals.astype(jnp.float32)[:, :, None], axis=1))
    unit_count = EXPERTS * FF // N_NARROW
    group_size = N_NARROW // EXPERTS
    block_count = unit_count // QBLOCK

    def add_slice(total, owner):
        piece_gu = lax.dynamic_slice_in_dim(gate_up, owner * unit_count, unit_count, 2)
        piece_q = lax.dynamic_slice_in_dim(quanta, owner * unit_count, unit_count, 1)
        piece_s = lax.dynamic_slice_in_dim(scales, owner * block_count, block_count, 1)
        partial_value = expert_rows(tokens, piece_gu, piece_q, piece_s).astype(jnp.bfloat16).astype(jnp.float32)
        column = owner // group_size
        chosen = (jnp.arange(EXPERTS, dtype=jnp.int32) == column).astype(jnp.float32)
        tok_weight = lax.optimization_barrier(jnp.sum(weights_tok * chosen[None, :], axis=1))
        return (total + tok_weight[:, None] * partial_value, None)
    start_total = jnp.zeros((tokens.shape[0], D), jnp.float32)
    combined = lax.scan(add_slice, start_total, jnp.arange(N_NARROW, dtype=jnp.int32))[0]
    return (new_master, new_one, new_two, combined.astype(jnp.bfloat16))
```

```python
import jax
import jax.numpy as jnp
from jax import lax
from jax.experimental import pallas as pl
from jax.experimental.pallas import tpu as pltpu
from jax.sharding import PartitionSpec as P

EXPERTS = 8
QBLOCK = 128
X, ZH, Y = 4, 2, 8
XZ = X * ZH
ZL = 6
CHUNKS = 8

beta_first = 0.9
beta_second = 0.95
learn_rate = 0.003
adam_eps = 1e-08
quant_limit = 448.0
amax_eps = 1e-06
bias_first = 1.0 - 0.9**10
bias_second = 1.0 - 0.95**10

VMEM = pl.BlockSpec(memory_space=pltpu.VMEM)
DMA = pltpu.SemaphoreType.DMA
f32 = jnp.float32
bf16 = jnp.bfloat16


def at_narrow(index):
    return {"narrow": index}


def at_wide(index):
    return {"wide": index}


def greet(partners):
    barrier = pltpu.get_barrier_semaphore()
    for where in partners:
        pl.semaphore_signal(barrier, inc=1, device_id=where, device_id_type=pl.DeviceIdType.MESH)
    pl.semaphore_wait(barrier, len(partners))


def remote(src, dst, send, recv, where):
    return pltpu.make_async_remote_copy(
        src_ref=src,
        dst_ref=dst,
        send_sem=send,
        recv_sem=recv,
        device_id=where,
        device_id_type=pl.DeviceIdType.MESH,
    )


def place():
    n = lax.axis_index("narrow")
    return n // (ZH * Y), (n // Y) % ZH, n % Y


def narrow_of(x, zh, y):
    return at_narrow((x * ZH + zh) * Y + y)


def gather_xz(own, landing, sems, x, zh, y):
    me = x * ZH + zh
    local = pltpu.make_async_copy(own, landing.at[me], sems.at[8])
    local.start()
    copy = remote(own, landing.at[me], sems.at[0], sems.at[1], narrow_of(x, 1 - zh, y))
    copy.start()
    local.wait()
    copy.wait()
    pair = landing.at[pl.ds(x * ZH, ZH)]
    copies = []
    for k in range(1, X):
        copies.append(
            remote(pair, pair, sems.at[1 + k], sems.at[4 + k], narrow_of((x + k) % X, zh, y))
        )
        copies[-1].start()
    for copy in copies:
        copy.wait()


def ring_y(blocks, right_send, right_recv, left_send, left_recv, x, zh, y):
    right = narrow_of(x, zh, (y + 1) % Y)
    left = narrow_of(x, zh, (y + Y - 1) % Y)
    for s in range(Y // 2):
        there = blocks.at[(y + Y - s) % Y]
        going = [remote(there, there, right_send.at[s], right_recv.at[s], right)]
        if s < Y // 2 - 1:
            there = blocks.at[(y + s) % Y]
            going.append(remote(there, there, left_send.at[s], left_recv.at[s], left))
        for copy in going:
            copy.start()
        for copy in going:
            copy.wait()


GATHER_SEMS = [DMA((9,)), DMA((4,)), DMA((4,)), DMA((3,)), DMA((3,))]


def partners_of(x, zh, y):
    found = [narrow_of(x, 1 - zh, y)]
    found += [narrow_of((x + k) % X, zh, y) for k in range(1, X)]
    return found + [narrow_of(x, zh, (y + k) % Y) for k in (1, Y - 1)]


def tokens_kernel(own_ref, out_ref, landing, wide_rows, sems, rs, rr, ls, lr):
    x, zh, y = place()
    greet(partners_of(x, zh, y))
    gather_xz(own_ref, landing, sems, x, zh, y)
    for j in range(XZ):
        for i in range(2):
            wide_rows[i * XZ + j : i * XZ + j + 1, :] = landing[j, i : i + 1, :].astype(f32)
    out_ref[pl.ds(y, 1)] = wide_rows[...].astype(bf16)[None]
    ring_y(out_ref, rs, rr, ls, lr, x, zh, y)


def hidden_kernel(own_ref, out_ref, sems, rs, rr, ls, lr):
    x, zh, y = place()
    greet(partners_of(x, zh, y))
    gather_xz(own_ref, out_ref.at[y], sems, x, zh, y)
    ring_y(out_ref, rs, rr, ls, lr, x, zh, y)


def grads_kernel(g_ref, out_ref, pre, land, part, ps, pr, is_, ir, os_, or_, cs, cr):
    w = lax.axis_index("wide")
    zl, core = w // 2, w % 2
    rows, columns = g_ref.shape
    half = columns // 2
    size = half // CHUNKS
    low = zl < ZL // 2
    edge = (zl == 0) | (zl == ZL - 1)
    mid = (zl == ZL // 2 - 1) | (zl == ZL // 2)
    inner = jnp.logical_not(edge | mid)
    inward = at_wide(jnp.where(low, w + 2, w - 2))
    outward = at_wide(jnp.where(edge, w, jnp.where(low, w - 2, w + 2)))
    other = at_wide(w + 1 - 2 * core)

    barrier = pltpu.get_barrier_semaphore()

    def signal(where):
        pl.semaphore_signal(barrier, inc=1, device_id=where, device_id_type=pl.DeviceIdType.MESH)

    signal(inward)
    signal(other)

    @pl.when(jnp.logical_not(edge))
    def _():
        signal(outward)

    pl.semaphore_wait(barrier, jnp.where(edge, 2, 3))

    def span(core_of, k):
        return pl.ds(pl.multiple_of(core_of * half + k * size, size), size)

    def here(k):
        return pl.ds(k * size, size)

    def pre_copy(k):
        return remote(g_ref.at[:, span(1 - core, k)], pre.at[:, here(k)], ps.at[k], pr.at[k], other)

    to_slot = jnp.where(mid, 1, 0)

    def in_copy(k, slot):
        return remote(part.at[:, here(k)], land.at[slot, :, here(k)], is_.at[k], ir.at[slot, k], inward)

    def out_copy(k):
        cut = out_ref.at[:, span(core, k)]
        return remote(cut, cut, os_.at[k], or_.at[k], outward)

    def core_copy(k, which):
        cut = out_ref.at[:, span(which, k)]
        return remote(cut, cut, cs.at[k], cr.at[k], other)

    for k in range(CHUNKS):
        pre_copy(k).start()

    def inbound(k):
        pre_copy(k).wait_recv()
        total = g_ref[:, span(core, k)].astype(f32) + pre[:, here(k)].astype(f32)

        @pl.when(edge)
        def _():
            part[:, here(k)] = total.astype(bf16)

        @pl.when(jnp.logical_not(edge))
        def _():
            in_copy(k, 0).wait_recv()
            part[:, here(k)] = (total + land[0, :, here(k)].astype(f32)).astype(bf16)

        in_copy(k, to_slot).start()

    def outbound_mid(k):
        in_copy(k, 1).wait_recv()
        total = part[:, here(k)].astype(f32) + land[1, :, here(k)].astype(f32)
        out_ref[:, span(core, k)] = total.astype(bf16)
        out_copy(k).start()
        core_copy(k, core).start()

    def outbound_inner(k):
        out_copy(k).wait_recv()
        out_copy(k).start()
        core_copy(k, core).start()

    def outbound_edge(k):
        out_copy(k).wait_recv()
        core_copy(k, core).start()

    for s in range(CHUNKS + 5):
        if s < CHUNKS:
            inbound(s)
        for role, lag, step in ((mid, 1, outbound_mid), (inner, 3, outbound_inner), (edge, 5, outbound_edge)):
            if 0 <= s - lag < CHUNKS:
                pl.when(role)(lambda step=step, k=s - lag: step(k))

    for k in range(CHUNKS):
        core_copy(k, 1 - core).wait_recv()
        pre_copy(k).wait_send()
        in_copy(k, to_slot).wait_send()
        core_copy(k, core).wait_send()

    @pl.when(jnp.logical_not(edge))
    def _():
        for k in range(CHUNKS):
            out_copy(k).wait_send()


def adam_kernel(g_ref, p_ref, one_ref, two_ref, hid_ref, newp_ref, newone_ref, newtwo_ref, comb_ref, acc):
    step = pl.program_id(0)
    rows = g_ref.shape[0]

    @pl.when(step == 0)
    def _():
        acc[...] = jnp.zeros_like(acc)

    total = acc[:rows, :]
    for b in range(Y):
        cut = slice(b * QBLOCK, (b + 1) * QBLOCK)
        grad = g_ref[:, cut].astype(f32)
        one = beta_first * one_ref[:, cut] + (1.0 - beta_first) * grad
        two = beta_second * two_ref[:, cut] + (1.0 - beta_second) * grad * grad
        newone_ref[:, cut] = one
        newtwo_ref[:, cut] = two
        step_dir = one * (1.0 / bias_first) / (jnp.sqrt(two * (1.0 / bias_second)) + adam_eps)
        updated = p_ref[:, cut].astype(f32) - learn_rate * step_dir
        newp_ref[:, cut] = updated.astype(bf16)
        amax = jnp.max(jnp.abs(updated), axis=1, keepdims=True)
        scale = ((amax + amax_eps) / quant_limit).astype(bf16).astype(f32)
        quanta = (updated * (1.0 / scale)).astype(bf16)
        total += scale * jnp.dot(quanta, hid_ref[b, 0], preferred_element_type=f32)
    acc[:rows, :] = total

    @pl.when(step == pl.num_programs(0) - 1)
    def _():
        turned = jnp.transpose(acc[...])
        for j in range(Y):
            first = turned[j * 16 : j * 16 + 8]
            second = turned[j * 16 + 8 : j * 16 + 16]
            comb_ref[j] = jnp.concatenate([first, second], axis=1)


def deliver_kernel(comb_ref, out_ref, first, turned, s1, r1, s2, r2):
    x, zh, y = place()
    me = x * ZH + zh
    partners = [narrow_of(x, zh, (y + k) % Y) for k in range(1, Y)]
    others = [(me + k) % XZ for k in range(1, XZ)]
    partners += [at_narrow(j * Y + y) for j in others]
    greet(partners)
    copies = []
    for k in range(1, Y):
        to = (y + k) % Y
        copies.append(remote(comb_ref.at[to], first.at[y], s1.at[k], r1.at[k], narrow_of(x, zh, to)))
        copies[-1].start()
    first[pl.ds(y, 1)] = comb_ref[pl.ds(y, 1)]
    for copy in copies:
        copy.wait()
    for j in range(Y):
        turned[:, j, :] = first[j]
    copies = []
    for k, to in enumerate(others):
        copies.append(remote(turned.at[to], out_ref.at[me], s2.at[k], r2.at[k], at_narrow(to * Y + y)))
        copies[-1].start()
    out_ref[pl.ds(me, 1)] = turned[pl.ds(me, 1)]
    for copy in copies:
        copy.wait()


def comm(kernel, out_shape, scratch, number):
    return pl.pallas_call(
        kernel,
        out_shape=out_shape,
        in_specs=[VMEM],
        out_specs=VMEM,
        scratch_shapes=scratch,
        compiler_params=pltpu.CompilerParams(
            collective_id=number, has_side_effects=True, vmem_limit_bytes=40 * 2**20
        ),
    )


def body(grad_parts, master, moment_one, moment_two, gate_up, tokens, expert_ids, gate_vals):
    shape = jax.ShapeDtypeStruct
    rows, columns = master.shape
    width = tokens.shape[1]
    onehot = expert_ids[:, :, None] == jnp.arange(EXPERTS, dtype=jnp.int32)[None, None, :]
    weights = jnp.sum(jnp.where(onehot, gate_vals.astype(f32)[:, :, None], 0.0), axis=1).astype(bf16)
    packed = jnp.concatenate([tokens, jnp.pad(weights, ((0, 0), (0, QBLOCK - EXPERTS)))], axis=1)
    full = width + QBLOCK
    gathered = comm(
        tokens_kernel,
        shape((Y, 16, full), bf16),
        [pltpu.VMEM((XZ, 2, full), bf16), pltpu.VMEM((16, full), f32)] + GATHER_SEMS,
        0,
    )(packed).reshape(Y * 16, full)

    proj = jnp.dot(gathered[:, :width], gate_up.reshape(width, 2 * QBLOCK), preferred_element_type=f32)
    expert = lax.axis_index("narrow") // Y
    chosen = jnp.arange(EXPERTS, dtype=jnp.int32) == expert
    weight = jnp.sum(jnp.where(chosen[None, :], gathered[:, width : width + EXPERTS].astype(f32), 0.0), axis=1)
    hidden = weight[:, None] * jax.nn.silu(proj[:, :QBLOCK]) * proj[:, QBLOCK:]
    hidden = hidden.astype(bf16).T
    tok = hidden.shape[1]
    hid_all = comm(hidden_kernel, shape((Y, XZ, QBLOCK, tok), bf16), GATHER_SEMS, 1)(hidden)

    half = columns // 2
    sem = DMA((CHUNKS,))
    grad = comm(
        grads_kernel,
        shape((rows, columns), bf16),
        [
            pltpu.VMEM((rows, half), bf16),
            pltpu.VMEM((2, rows, half), bf16),
            pltpu.VMEM((rows, half), bf16),
            sem, sem, sem, DMA((2, CHUNKS)), sem, sem, sem, sem,
        ],
        2,
    )(grad_parts[0])

    part = columns // EXPERTS
    spec = pl.BlockSpec((rows, part), lambda e: (0, e))
    new_master, new_one, new_two, comb = pl.pallas_call(
        adam_kernel,
        grid=(EXPERTS,),
        out_shape=(
            shape((rows, columns), bf16),
            shape((rows, columns), f32),
            shape((rows, columns), f32),
            shape((Y, XZ, 128), f32),
        ),
        in_specs=[spec, spec, spec, spec, pl.BlockSpec((Y, 1, QBLOCK, tok), lambda e: (0, e, 0, 0))],
        out_specs=(spec, spec, spec, pl.BlockSpec((Y, XZ, 128), lambda e: (0, 0, 0))),
        scratch_shapes=[pltpu.VMEM((64, tok), f32)],
        compiler_params=pltpu.CompilerParams(vmem_limit_bytes=40 * 2**20),
    )(grad, master, moment_one, moment_two, hid_all)

    tile = pltpu.VMEM((8, 8, 128), f32)
    done = comm(
        deliver_kernel,
        shape((XZ, Y, 128), f32),
        [tile, tile, DMA((8,)), DMA((8,)), DMA((8,)), DMA((8,))],
        3,
    )(comb)
    done = done.reshape(XZ, Y, 2, 64)[..., :rows].transpose(2, 0, 1, 3).reshape(2, width)
    return new_master, new_one, new_two, done.astype(bf16)


def solution(mesh):
    in_specs = (
        P("wide", "narrow", None),
        P("narrow", None),
        P("narrow", None),
        P("narrow", None),
        P(None, None, "narrow"),
        P(("wide", "narrow"), None),
        P(("wide", "narrow"), None),
        P(("wide", "narrow"), None),
    )
    out_specs = (
        P("narrow", None),
        P("narrow", None),
        P("narrow", None),
        P(("wide", "narrow"), None),
    )
    return jax.shard_map(body, mesh=mesh, in_specs=in_specs, out_specs=out_specs, check_vma=False)
```

```python
import jax
import jax.numpy as jnp
from jax import lax
from jax.experimental import pallas as pl
from jax.experimental.pallas import tpu as pltpu
from jax.sharding import PartitionSpec as P

EXPERTS = 8
QBLOCK = 128
X, ZH, Y = 4, 2, 8
XZ = X * ZH
ZL = 6
CHUNKS = 8

beta_first = 0.9
beta_second = 0.95
learn_rate = 0.003
adam_eps = 1e-08
quant_limit = 448.0
amax_eps = 1e-06
bias_first = 1.0 - 0.9**10
bias_second = 1.0 - 0.95**10

VMEM = pl.BlockSpec(memory_space=pltpu.VMEM)
DMA = pltpu.SemaphoreType.DMA
f32 = jnp.float32
bf16 = jnp.bfloat16


def at_wide(index):
    return {"wide": index}


def remote(src, dst, send, recv, where):
    return pltpu.make_async_remote_copy(
        src_ref=src,
        dst_ref=dst,
        send_sem=send,
        recv_sem=recv,
        device_id=where,
        device_id_type=pl.DeviceIdType.MESH,
    )


def signal(where):
    pl.semaphore_signal(
        pltpu.get_barrier_semaphore(), inc=1, device_id=where, device_id_type=pl.DeviceIdType.MESH
    )


def place():
    n = lax.axis_index("narrow")
    return n // (ZH * Y), (n // Y) % ZH, n % Y


def device(x, zh, y):
    w = lax.axis_index("wide")
    own = (lax.axis_index("narrow") // Y) % ZH
    mirrored = (ZL - 1 - w // 2) * 2 + w % 2
    return {"wide": jnp.where(zh == own, w, mirrored), "narrow": (x * ZH + zh) * Y + y}


GATHER_SEMS = [DMA((9,))]
RING_SEMS = [DMA((4,)), DMA((4,)), DMA((4,)), DMA((4,))]


class Gather:
    def __init__(self, own, landing, sems):
        x, zh, y = place()
        me = x * ZH + zh
        self.local = pltpu.make_async_copy(own, landing.at[me], sems.at[8])
        self.cross = remote(own, landing.at[me], sems.at[0], sems.at[1], device(x, 1 - zh, y))
        pair = landing.at[pl.ds(x * ZH, ZH)]
        self.along = [
            remote(pair, pair, sems.at[1 + k], sems.at[4 + k], device((x + k) % X, zh, y))
            for k in range(1, X)
        ]

    def start(self):
        self.cross.start()
        self.local.start()

    def turn(self):
        self.local.wait()
        self.cross.wait()
        for copy in self.along:
            copy.start()

    def finish(self):
        for copy in self.along:
            copy.wait()


class Ring:
    def __init__(self, blocks, cut, right_send, right_recv, left_send, left_recv):
        x, zh, y = place()
        right, left = device(x, zh, (y + 1) % Y), device(x, zh, (y + Y - 1) % Y)
        self.steps = []
        for s in range(Y // 2):
            first, second = blocks.at[(y + Y - s) % Y], blocks.at[(y + s) % Y]
            if s == Y // 2 - 1:
                first, second = first.at[:, :cut], second.at[:, cut:]
            self.steps.append(
                (
                    remote(first, first, right_send.at[s], right_recv.at[s], right),
                    remote(second, second, left_send.at[s], left_recv.at[s], left),
                )
            )

    def start(self, s):
        for copy in self.steps[s]:
            copy.start()

    def wait(self, s):
        for copy in self.steps[s]:
            copy.wait()


class Sum:
    def __init__(self, g_ref, out_ref, pre, land, part, ps, pr, is_, ir, os_, or_, cs, cr):
        w = lax.axis_index("wide")
        zl, core = w // 2, w % 2
        half = g_ref.shape[1] // 2
        size = half // CHUNKS
        low = zl < ZL // 2
        edge = (zl == 0) | (zl == ZL - 1)
        mid = (zl == ZL // 2 - 1) | (zl == ZL // 2)
        inward = at_wide(jnp.where(low, w + 2, w - 2))
        outward = at_wide(jnp.where(edge, w, jnp.where(low, w - 2, w + 2)))
        other = at_wide(w + 1 - 2 * core)
        self.edge, self.mid, self.inner = edge, mid, jnp.logical_not(edge | mid)
        self.core, self.inward, self.outward, self.other = core, inward, outward, other
        self.g_ref, self.out_ref, self.pre, self.land, self.part = g_ref, out_ref, pre, land, part

        def span(core_of, k):
            return pl.ds(pl.multiple_of(core_of * half + k * size, size), size)

        def here(k):
            return pl.ds(k * size, size)

        def pre_copy(k):
            src = g_ref.at[:, span(1 - core, k)]
            return remote(src, pre.at[:, here(k)], ps.at[k], pr.at[k], other)

        def in_copy(k, slot):
            dst = land.at[slot, :, here(k)]
            return remote(part.at[:, here(k)], dst, is_.at[k], ir.at[slot, k], inward)

        def out_copy(k):
            cut = out_ref.at[:, span(core, k)]
            return remote(cut, cut, os_.at[k], or_.at[k], outward)

        def core_copy(k, which):
            cut = out_ref.at[:, span(which, k)]
            return remote(cut, cut, cs.at[k], cr.at[k], other)

        self.span, self.here = span, here
        self.pre_copy, self.in_copy, self.out_copy, self.core_copy = pre_copy, in_copy, out_copy, core_copy
        self.to_slot = jnp.where(mid, 1, 0)

    def greet(self):
        signal(self.inward)
        signal(self.other)
        pl.when(jnp.logical_not(self.edge))(lambda: signal(self.outward))
        return jnp.where(self.edge, 2, 3)

    def start(self):
        for k in range(CHUNKS):
            self.pre_copy(k).start()

    def inbound(self, k):
        self.pre_copy(k).wait_recv()
        here = self.here(k)
        total = self.g_ref[:, self.span(self.core, k)].astype(f32) + self.pre[:, here].astype(f32)

        @pl.when(self.edge)
        def _():
            self.part[:, here] = total.astype(bf16)

        @pl.when(jnp.logical_not(self.edge))
        def _():
            self.in_copy(k, 0).wait_recv()
            self.part[:, here] = (total + self.land[0, :, here].astype(f32)).astype(bf16)

        self.in_copy(k, self.to_slot).start()

    def outbound_mid(self, k):
        self.in_copy(k, 1).wait_recv()
        total = self.part[:, self.here(k)].astype(f32) + self.land[1, :, self.here(k)].astype(f32)
        self.out_ref[:, self.span(self.core, k)] = total.astype(bf16)
        self.out_copy(k).start()
        self.core_copy(k, self.core).start()

    def outbound_inner(self, k):
        self.out_copy(k).wait_recv()
        self.out_copy(k).start()
        self.core_copy(k, self.core).start()

    def outbound_edge(self, k):
        self.out_copy(k).wait_recv()
        self.core_copy(k, self.core).start()

    def step(self, s):
        if s < CHUNKS:
            self.inbound(s)
        for role, lag, run in (
            (self.mid, 1, self.outbound_mid),
            (self.inner, 3, self.outbound_inner),
            (self.edge, 5, self.outbound_edge),
        ):
            if 0 <= s - lag < CHUNKS:
                pl.when(role)(lambda run=run, k=s - lag: run(k))

    def finish(self):
        for k in range(CHUNKS):
            self.core_copy(k, 1 - self.core).wait_recv()
            self.pre_copy(k).wait_send()
            self.in_copy(k, self.to_slot).wait_send()
            self.core_copy(k, self.core).wait_send()

        @pl.when(jnp.logical_not(self.edge))
        def _():
            for k in range(CHUNKS):
                self.out_copy(k).wait_send()


def first_kernel(own_ref, g_ref, out_ref, sum_ref, landing, wide_rows, sems, rs, rr, ls, lr, *rest):
    x, zh, y = place()
    adding = Sum(g_ref, sum_ref, *rest)
    count = adding.greet()
    partners = [device(x, 1 - zh, y)]
    partners += [device((x + k) % X, zh, y) for k in range(1, X)]
    partners += [device(x, zh, (y + k) % Y) for k in (1, Y - 1)]
    for where in partners:
        signal(where)
    pl.semaphore_wait(pltpu.get_barrier_semaphore(), count + len(partners))

    gather = Gather(own_ref, landing, sems)
    width = own_ref.shape[1]
    ring = Ring(out_ref, width // 256 * 128, rs, rr, ls, lr)
    gather.start()
    adding.start()
    adding.step(0)
    adding.step(1)
    gather.turn()
    adding.step(2)
    adding.step(3)
    gather.finish()
    for j in range(XZ):
        for i in range(2):
            wide_rows[i * XZ + j : i * XZ + j + 1, :] = landing[j, i : i + 1, :].astype(f32)
    out_ref[pl.ds(y, 1)] = wide_rows[...].astype(bf16)[None]
    ring.start(0)
    for s in range(Y // 2):
        adding.step(4 + 2 * s)
        adding.step(5 + 2 * s)
        ring.wait(s)
        if s + 1 < Y // 2:
            ring.start(s + 1)
    for s in range(12, CHUNKS + 5):
        adding.step(s)
    adding.finish()


def adam_kernel(g_ref, p_ref, one_ref, two_ref, newp_ref, newone_ref, newtwo_ref, q_ref):
    step = pl.program_id(0)
    rows = g_ref.shape[0]
    half = EXPERTS // 2
    lane = lax.broadcasted_iota(jnp.int32, (rows, QBLOCK), 1)
    spot = step % half
    for b in range(Y):
        cut = slice(b * QBLOCK, (b + 1) * QBLOCK)
        grad = g_ref[:, cut].astype(f32)
        one = beta_first * one_ref[:, cut] + (1.0 - beta_first) * grad
        two = beta_second * two_ref[:, cut] + (1.0 - beta_second) * grad * grad
        newone_ref[:, cut] = one
        newtwo_ref[:, cut] = two
        step_dir = one * (1.0 / bias_first) / (jnp.sqrt(two * (1.0 / bias_second)) + adam_eps)
        updated = p_ref[:, cut].astype(f32) - learn_rate * step_dir
        newp_ref[:, cut] = updated.astype(bf16)
        amax = jnp.max(jnp.abs(updated), axis=1, keepdims=True)
        scale = ((amax + amax_eps) / quant_limit).astype(bf16).astype(f32)
        q_ref[0, b, :, pl.ds(pl.multiple_of(spot * QBLOCK, QBLOCK), QBLOCK)] = (
            updated * (1.0 / scale)
        ).astype(bf16)
        held = q_ref[0, b, :, half * QBLOCK :].astype(f32)
        held = jnp.where((spot == 0) | (lane > spot), 0.0, held)
        q_ref[0, b, :, half * QBLOCK :] = jnp.where(lane == spot, scale, held).astype(bf16)


def second_kernel(
    hid_ref, q_ref, out_ref, hid_all, rows_all, acc, sent, came, turned,
    sems, ys, yr, cs, cr, s1, r1, s2, r2,
):
    x, zh, y = place()
    w = lax.axis_index("wide")
    core = w % 2
    me = x * ZH + zh
    half = EXPERTS // 2
    rows = q_ref.shape[2]
    other = at_wide(w + 1 - 2 * core)
    column = [device(x, zh, (y + k) % Y) for k in range(1, Y)]
    plane = []
    for k in range(1, XZ):
        to = (me + k) % XZ
        plane.append(device(to // ZH, to % ZH, y))
    for where in column + plane + [other]:
        signal(where)
    pl.semaphore_wait(pltpu.get_barrier_semaphore(), len(column) + len(plane) + 1)

    gather = Gather(hid_ref, hid_all, sems)
    gather.start()
    relays = [
        remote(
            q_ref.at[core, (y + k) % Y], rows_all.at[core, y], ys.at[k], yr.at[k], column[k - 1]
        )
        for k in range(1, Y)
    ]
    order = [1, 7, 2, 6, 3, 5, 4]
    for k in order:
        relays[k - 1].start()
    mine = pltpu.make_async_copy(q_ref.at[core, y], rows_all.at[core, y], ys.at[0])
    mine.start()

    def share(k, which):
        part = rows_all.at[which, (y + Y - k) % Y]
        return remote(part, part, cs.at[k], cr.at[k], other)

    mine.wait()
    share(0, core).start()
    gather.turn()
    for k in order:
        relays[k - 1].wait_recv()
        share(k, core).start()
    gather.finish()

    def products(which, block):
        total = jnp.zeros((rows, hid_ref.shape[1]), f32)
        for e in range(half):
            quanta = rows_all[which, block, :, e * QBLOCK : (e + 1) * QBLOCK]
            scale = rows_all[which, block, :, half * QBLOCK + e : half * QBLOCK + e + 1].astype(f32)
            total += scale * jnp.dot(quanta, hid_all[which * half + e], preferred_element_type=f32)
        return total

    for j in range(Y):
        acc[j, :rows] = products(core, j)
    for k in [0] + order:
        share(k, 1 - core).wait_recv()
    for j in range(Y):
        acc[j, :rows] += products(1 - core, j)
        acc[j, rows:] = jnp.zeros_like(acc[j, rows:])
    for j in range(Y // 2):
        pair = jnp.concatenate([acc[2 * j], acc[2 * j + 1]], axis=0)
        pair = jnp.transpose(pair).astype(bf16)
        for t in range(Y):
            sent[t, :, j * QBLOCK : (j + 1) * QBLOCK] = pair[t * 16 : (t + 1) * 16]

    copies = []
    for k in order:
        to = (y + k) % Y
        copies.append(remote(sent.at[to], came.at[y], s1.at[k], r1.at[k], column[k - 1]))
        copies[-1].start()
    came[pl.ds(y, 1)] = sent[pl.ds(y, 1)]
    for copy in copies:
        copy.wait()
    total = came[0].astype(f32)
    for j in range(1, Y):
        total += came[j].astype(f32)
    for i in range(2):
        for q in range(4):
            turned[:, i * 4 + q, :] = total[i * 8 : (i + 1) * 8, q * 128 : (q + 1) * 128]
    copies = []
    for k in range(1, XZ):
        to = (me + k) % XZ
        copies.append(remote(turned.at[to], out_ref.at[me], s2.at[k], r2.at[k], plane[k - 1]))
        copies[-1].start()
    out_ref[pl.ds(me, 1)] = turned[pl.ds(me, 1)]
    for copy in copies:
        copy.wait()
    for k in order:
        relays[k - 1].wait_send()
    for k in range(Y):
        share(k, core).wait_send()


def comm(kernel, out_shape, scratch, number, inputs):
    return pl.pallas_call(
        kernel,
        out_shape=out_shape,
        in_specs=[VMEM] * inputs,
        out_specs=VMEM if not isinstance(out_shape, tuple) else (VMEM,) * len(out_shape),
        scratch_shapes=scratch,
        compiler_params=pltpu.CompilerParams(
            collective_id=number, has_side_effects=True, vmem_limit_bytes=40 * 2**20
        ),
    )


def body(grad_parts, master, moment_one, moment_two, gate_up, tokens, expert_ids, gate_vals):
    shape = jax.ShapeDtypeStruct
    rows, columns = master.shape
    width = tokens.shape[1]
    onehot = expert_ids[:, :, None] == jnp.arange(EXPERTS, dtype=jnp.int32)[None, None, :]
    weights = jnp.sum(jnp.where(onehot, gate_vals.astype(f32)[:, :, None], 0.0), axis=1).astype(bf16)
    packed = jnp.concatenate([tokens, jnp.pad(weights, ((0, 0), (0, QBLOCK - EXPERTS)))], axis=1)
    full = width + QBLOCK
    half = columns // 2
    sem = DMA((CHUNKS,))
    gathered, grad = comm(
        first_kernel,
        (shape((Y, 16, full), bf16), shape((rows, columns), bf16)),
        [pltpu.VMEM((XZ, 2, full), bf16), pltpu.VMEM((16, full), f32)]
        + GATHER_SEMS
        + RING_SEMS
        + [
            pltpu.VMEM((rows, half), bf16),
            pltpu.VMEM((2, rows, half), bf16),
            pltpu.VMEM((rows, half), bf16),
            sem, sem, sem, DMA((2, CHUNKS)), sem, sem, sem, sem,
        ],
        0,
        2,
    )(packed, grad_parts[0])
    gathered = gathered.reshape(Y * 16, full)

    proj = jnp.dot(gathered[:, :width], gate_up.reshape(width, 2 * QBLOCK), preferred_element_type=f32)
    expert = lax.axis_index("narrow") // Y
    chosen = jnp.arange(EXPERTS, dtype=jnp.int32) == expert
    weight = jnp.sum(jnp.where(chosen[None, :], gathered[:, width : width + EXPERTS].astype(f32), 0.0), axis=1)
    hidden = weight[:, None] * jax.nn.silu(proj[:, :QBLOCK]) * proj[:, QBLOCK:]
    hidden = hidden.astype(bf16).T
    tok = hidden.shape[1]

    part = columns // EXPERTS
    spec = pl.BlockSpec((rows, part), lambda e: (0, e))
    per = EXPERTS // 2
    lanes = (per + 1) * QBLOCK
    new_master, new_one, new_two, quanta = pl.pallas_call(
        adam_kernel,
        grid=(EXPERTS,),
        out_shape=(
            shape((rows, columns), bf16),
            shape((rows, columns), f32),
            shape((rows, columns), f32),
            shape((2, Y, rows, lanes), bf16),
        ),
        in_specs=[spec, spec, spec, spec],
        out_specs=(spec, spec, spec, pl.BlockSpec((1, Y, rows, lanes), lambda e: (e // per, 0, 0, 0))),
        compiler_params=pltpu.CompilerParams(vmem_limit_bytes=40 * 2**20),
    )(grad, master, moment_one, moment_two)

    sems = DMA((8,))
    done = comm(
        second_kernel,
        shape((XZ, Y, 128), f32),
        [
            pltpu.VMEM((XZ, QBLOCK, tok), bf16),
            pltpu.VMEM((2, Y, rows, lanes), bf16),
            pltpu.VMEM((Y, 64, tok), f32),
            pltpu.VMEM((Y, 16, 512), bf16),
            pltpu.VMEM((Y, 16, 512), bf16),
            pltpu.VMEM((XZ, 8, 128), f32),
        ]
        + GATHER_SEMS
        + [sems] * 8,
        1,
        2,
    )(hidden, quanta)
    done = done.reshape(XZ, 2, Y, 64)[..., :rows].transpose(1, 0, 2, 3).reshape(2, width)
    return new_master, new_one, new_two, done.astype(bf16)


def solution(mesh):
    in_specs = (
        P("wide", "narrow", None),
        P("narrow", None),
        P("narrow", None),
        P("narrow", None),
        P(None, None, "narrow"),
        P(("wide", "narrow"), None),
        P(("wide", "narrow"), None),
        P(("wide", "narrow"), None),
    )
    out_specs = (
        P("narrow", None),
        P("narrow", None),
        P("narrow", None),
        P(("wide", "narrow"), None),
    )
    return jax.shard_map(body, mesh=mesh, in_specs=in_specs, out_specs=out_specs, check_vma=False)
```

```python
import jax
import jax.numpy as jnp
from jax import lax
from jax.experimental import pallas as pl
from jax.experimental.pallas import tpu as pltpu
from jax.sharding import PartitionSpec as P

EXPERTS = 8
QBLOCK = 128
X, ZH, Y = 4, 2, 8
XZ = X * ZH
ZL = 6
CHUNKS = 4

beta_first = 0.9
beta_second = 0.95
learn_rate = 0.003
adam_eps = 1e-08
quant_limit = 448.0
amax_eps = 1e-06
bias_first = 1.0 - 0.9**10
bias_second = 1.0 - 0.95**10

VMEM = pl.BlockSpec(memory_space=pltpu.VMEM)
ANY = pl.BlockSpec(memory_space=pl.ANY)
DMA = pltpu.SemaphoreType.DMA
f32 = jnp.float32
bf16 = jnp.bfloat16


def at_wide(index):
    return {"wide": index}


def remote(src, dst, send, recv, where):
    return pltpu.make_async_remote_copy(
        src_ref=src,
        dst_ref=dst,
        send_sem=send,
        recv_sem=recv,
        device_id=where,
        device_id_type=pl.DeviceIdType.MESH,
    )


def signal(where):
    pl.semaphore_signal(
        pltpu.get_barrier_semaphore(), inc=1, device_id=where, device_id_type=pl.DeviceIdType.MESH
    )


def place():
    n = lax.axis_index("narrow")
    return n // (ZH * Y), (n // Y) % ZH, n % Y


def device(x, zh, y):
    w = lax.axis_index("wide")
    own = (lax.axis_index("narrow") // Y) % ZH
    mirrored = (ZL - 1 - w // 2) * 2 + w % 2
    return {"wide": jnp.where(zh == own, w, mirrored), "narrow": (x * ZH + zh) * Y + y}


GATHER_SEMS = [DMA((9,))]
RING_SEMS = [DMA((4,)), DMA((4,)), DMA((4,)), DMA((4,))]


class Gather:
    def __init__(self, own, landing, sems):
        x, zh, y = place()
        me = x * ZH + zh
        self.local = pltpu.make_async_copy(own, landing.at[me], sems.at[8])
        self.cross = remote(own, landing.at[me], sems.at[0], sems.at[1], device(x, 1 - zh, y))
        pair = landing.at[pl.ds(x * ZH, ZH)]
        self.along = [
            remote(pair, pair, sems.at[1 + k], sems.at[4 + k], device((x + k) % X, zh, y))
            for k in range(1, X)
        ]

    def start(self):
        self.cross.start()
        self.local.start()

    def turn(self):
        self.local.wait()
        self.cross.wait()
        for copy in self.along:
            copy.start()

    def finish(self):
        for copy in self.along:
            copy.wait()


class Ring:
    def __init__(self, blocks, cut, right_send, right_recv, left_send, left_recv):
        x, zh, y = place()
        right, left = device(x, zh, (y + 1) % Y), device(x, zh, (y + Y - 1) % Y)
        self.steps = []
        for s in range(Y // 2):
            first, second = blocks.at[(y + Y - s) % Y], blocks.at[(y + s) % Y]
            if s == Y // 2 - 1:
                first, second = first.at[:, :cut], second.at[:, cut:]
            self.steps.append(
                (
                    remote(first, first, right_send.at[s], right_recv.at[s], right),
                    remote(second, second, left_send.at[s], left_recv.at[s], left),
                )
            )

    def start(self, s):
        for copy in self.steps[s]:
            copy.start()

    def wait(self, s):
        for copy in self.steps[s]:
            copy.wait()


class Sum:
    def __init__(self, g_ref, out_ref, own, pre, land, part, ld, ps, pr, is_, ir, os_, or_, cs, cr):
        w = lax.axis_index("wide")
        zl, core = w // 2, w % 2
        half = g_ref.shape[1] // 2
        size = half // CHUNKS
        low = zl < ZL // 2
        edge = (zl == 0) | (zl == ZL - 1)
        mid = (zl == ZL // 2 - 1) | (zl == ZL // 2)
        inward = at_wide(jnp.where(low, w + 2, w - 2))
        outward = at_wide(jnp.where(edge, w, jnp.where(low, w - 2, w + 2)))
        other = at_wide(w + 1 - 2 * core)
        self.edge, self.mid, self.inner = edge, mid, jnp.logical_not(edge | mid)
        self.core, self.inward, self.outward, self.other = core, inward, outward, other
        self.out_ref, self.own, self.pre, self.land, self.part = out_ref, own, pre, land, part
        self.to_slot = jnp.where(mid, 1, 0)

        def span(core_of, k):
            return pl.ds(pl.multiple_of(core_of * half + k * size, size), size)

        def load(k):
            return pltpu.make_async_copy(g_ref.at[:, span(core, k)], own.at[k], ld.at[k])

        def pre_copy(k):
            return remote(g_ref.at[:, span(1 - core, k)], pre.at[k], ps.at[k], pr.at[k], other)

        def in_copy(k, slot):
            return remote(part.at[k], land.at[slot, k], is_.at[k], ir.at[slot, k], inward)

        def out_copy(k):
            cut = out_ref.at[core, k]
            return remote(cut, cut, os_.at[k], or_.at[k], outward)

        def core_copy(k, which):
            cut = out_ref.at[which, k]
            return remote(cut, cut, cs.at[k], cr.at[k], other)

        self.load, self.pre_copy, self.in_copy, self.out_copy, self.core_copy = (
            load, pre_copy, in_copy, out_copy, core_copy,
        )

    def greet(self):
        signal(self.inward)
        signal(self.other)
        pl.when(jnp.logical_not(self.edge))(lambda: signal(self.outward))
        return jnp.where(self.edge, 2, 3)

    def start(self):
        for k in range(CHUNKS):
            self.pre_copy(k).start()

    def inbound(self, k):
        self.load(k).wait()
        self.pre_copy(k).wait_recv()

        @pl.when(self.edge)
        def _():
            self.part[k] = (self.own[k].astype(f32) + self.pre[k].astype(f32)).astype(bf16)

        @pl.when(jnp.logical_not(self.edge))
        def _():
            self.in_copy(k, 0).wait_recv()
            total = self.own[k].astype(f32) + self.pre[k].astype(f32)
            self.part[k] = (total + self.land[0, k].astype(f32)).astype(bf16)

        self.in_copy(k, self.to_slot).start()

    def middle(self, k):
        @pl.when(self.mid)
        def _():
            self.in_copy(k, 1).wait_recv()
            total = self.part[k].astype(f32) + self.land[1, k].astype(f32)
            self.out_ref[pl.ds(self.core, 1), k] = total.astype(bf16)[None]
            self.out_copy(k).start()
            self.core_copy(k, self.core).start()

    def inner_out(self, k):
        @pl.when(self.inner)
        def _():
            self.out_copy(k).wait_recv()
            self.out_copy(k).start()
            self.core_copy(k, self.core).start()

    def edge_out(self, k):
        @pl.when(self.edge)
        def _():
            self.out_copy(k).wait_recv()
            self.core_copy(k, self.core).start()

    def finish(self):
        for k in range(CHUNKS):
            self.core_copy(k, 1 - self.core).wait_recv()
            self.pre_copy(k).wait_send()
            self.in_copy(k, self.to_slot).wait_send()
            self.core_copy(k, self.core).wait_send()

        @pl.when(jnp.logical_not(self.edge))
        def _():
            for k in range(CHUNKS):
                self.out_copy(k).wait_send()


def adam(grad, master, moment_one, moment_two):
    one = beta_first * moment_one + (1.0 - beta_first) * grad
    two = beta_second * moment_two + (1.0 - beta_second) * grad * grad
    step_dir = one * (1.0 / bias_first) / (jnp.sqrt(two * (1.0 / bias_second)) + adam_eps)
    return one, two, master - learn_rate * step_dir


def main_kernel(
    tok_ref, ids_ref, gate_ref, g_ref, p_ref, one_ref, two_ref, w_ref,
    sum_ref, out_ref,
    own, landing, wide_rows, gathered, w_raw, w_tmp, w_both,
    p_half, one_half, two_half, q_send, rows_all, hid_own, hid_all, acc, sent, came, turned, both,
    ld, sems, rs, rr, ls, lr, hsems, ys, yr, cs, cr, s1, r1, s2, r2, *rest
):
    x, zh, y = place()
    w = lax.axis_index("wide")
    core = w % 2
    other = at_wide(w + 1 - 2 * core)
    expert = x * ZH + zh
    rows, columns = p_ref.shape
    half = columns // 2
    width = tok_ref.shape[1]
    per = EXPERTS // 2
    batches, fit = 2, per // 2
    adding = Sum(g_ref, sum_ref, *rest)

    count = adding.greet()
    column = [device(x, zh, (y + k) % Y) for k in range(1, Y)]
    near = [device(x, 1 - zh, y)] + [device((x + k) % X, zh, y) for k in range(1, X)]
    for where in column + near:
        signal(where)

    span = pl.ds(pl.multiple_of(core * half, half), half)
    w_load = pltpu.make_async_copy(w_ref, w_raw, ld.at[0])
    state_loads = [
        pltpu.make_async_copy(p_ref.at[:, span], p_half, ld.at[1]),
        pltpu.make_async_copy(one_ref.at[:, span], one_half, ld.at[2]),
        pltpu.make_async_copy(two_ref.at[:, span], two_half, ld.at[3]),
    ]
    for k in range(CHUNKS):
        adding.load(k).start()
    w_load.start()
    for copy in state_loads:
        copy.start()

    own[:, :width] = tok_ref[...]
    lane = lax.broadcasted_iota(jnp.int32, (2, QBLOCK), 1)
    weights = jnp.zeros((2, QBLOCK), f32)
    for k in range(ids_ref.shape[1]):
        gate = gate_ref[:, k : k + 1].astype(f32)
        weights += jnp.where(ids_ref[:, k : k + 1] == lane, gate, 0.0)
    own[:, width:] = weights.astype(bf16)
    pl.semaphore_wait(pltpu.get_barrier_semaphore(), count + len(column) + len(near))

    gather = Gather(own, landing, sems)
    ring = Ring(gathered, own.shape[1] // 256 * 128, rs, rr, ls, lr)
    gather.start()
    adding.start()

    w_load.wait()
    piece = w_tmp.shape[0]

    def split(i, carry):
        w_tmp[...] = w_raw[pl.ds(pl.multiple_of(i * piece, piece), piece), :].astype(f32)
        to = pl.ds(pl.multiple_of(i * (piece // 2), piece // 2), piece // 2)
        w_both[to, :QBLOCK] = w_tmp[pl.ds(0, piece // 2, stride=2), :].astype(bf16)
        w_both[to, QBLOCK:] = w_tmp[pl.ds(1, piece // 2, stride=2), :].astype(bf16)
        return carry

    lax.fori_loop(0, w_raw.shape[0] // piece, split, 0)

    gather.turn()
    adding.inbound(0)
    gather.finish()
    for j in range(XZ):
        for i in range(2):
            wide_rows[i * XZ + j : i * XZ + j + 1, :] = landing[j, i : i + 1, :].astype(f32)
    gathered[pl.ds(y, 1)] = wide_rows[...].astype(bf16)[None]
    ring.start(0)
    for copy in state_loads:
        copy.wait()

    def quantize(k):
        batch, spot = k // fit, k % fit
        for b in range(Y):
            cut = slice(k * Y * QBLOCK + b * QBLOCK, k * Y * QBLOCK + (b + 1) * QBLOCK)
            grad = sum_ref[core, k, :, b * QBLOCK : (b + 1) * QBLOCK].astype(f32)
            _, _, updated = adam(grad, p_half[:, cut].astype(f32), one_half[:, cut], two_half[:, cut])
            amax = jnp.max(jnp.abs(updated), axis=1, keepdims=True)
            scale = ((amax + amax_eps) / quant_limit).astype(bf16)
            quanta = (updated * (1.0 / scale.astype(f32))).astype(bf16)
            q_send[batch, b, :, spot * QBLOCK : (spot + 1) * QBLOCK] = quanta
            q_send[batch, b, :, fit * QBLOCK + spot : fit * QBLOCK + spot + 1] = scale

    order = [1, 7, 2, 6, 3, 5, 4]

    def relay(batch, k):
        return remote(
            q_send.at[batch, (y + k) % Y], rows_all.at[core, batch, y],
            ys.at[batch, k], yr.at[batch, k], column[k - 1],
        )

    def mine(batch):
        return pltpu.make_async_copy(
            q_send.at[batch, y], rows_all.at[core, batch, y], ys.at[batch, 0]
        )

    def relay_start(batch):
        for k in order:
            relay(batch, k).start()
        mine(batch).start()

    def share(batch, which):
        part = rows_all.at[which, batch]
        return remote(part, part, cs.at[batch], cr.at[batch], other)

    def relay_finish(batch):
        mine(batch).wait()
        for k in order:
            relay(batch, k).wait_recv()
        share(batch, core).start()

    adding.inbound(1)
    adding.inbound(2)
    adding.middle(0)
    ring.wait(0)
    ring.start(1)
    adding.inbound(3)
    adding.middle(1)
    adding.middle(2)
    adding.inner_out(0)
    ring.wait(1)
    ring.start(2)
    adding.middle(3)
    adding.inner_out(1)
    adding.inner_out(2)
    adding.edge_out(0)
    ring.wait(2)
    ring.start(3)
    quantize(0)
    adding.inner_out(3)
    adding.edge_out(1)
    quantize(1)
    relay_start(0)
    adding.edge_out(2)
    ring.wait(3)

    tokens = gathered.reshape(Y * 16, own.shape[1])
    proj = jnp.dot(tokens[:, :width], w_both[...], preferred_element_type=f32)
    weight = tokens[:, width:].astype(f32)
    lanes = lax.broadcasted_iota(jnp.int32, weight.shape, 1)
    weight = jnp.sum(jnp.where(lanes == expert, weight, 0.0), axis=1, keepdims=True)
    gate = proj[:, :QBLOCK]
    hidden = weight * (gate * jax.nn.sigmoid(gate)) * proj[:, QBLOCK:]
    hid_own[...] = jnp.transpose(hidden).astype(bf16)
    hid_gather = Gather(hid_own, hid_all, hsems)
    hid_gather.start()
    adding.edge_out(3)
    quantize(2)
    quantize(3)
    relay_start(1)
    relay_finish(0)
    hid_gather.turn()
    relay_finish(1)
    hid_gather.finish()

    def products(which, batch):
        for j in range(Y):
            total = None
            for e in range(fit):
                quanta = rows_all[which, batch, j, :, e * QBLOCK : (e + 1) * QBLOCK]
                scale = rows_all[which, batch, j, :, fit * QBLOCK + e : fit * QBLOCK + e + 1]
                term = scale.astype(f32) * jnp.dot(
                    quanta, hid_all[which * per + batch * fit + e], preferred_element_type=f32
                )
                total = term if total is None else total + term
            yield j, total

    for j, total in products(core, 0):
        acc[j, :rows] = total
        acc[j, rows:] = jnp.zeros_like(acc[j, rows:])
    for j, total in products(core, 1):
        acc[j, :rows] += total
    for batch in range(batches):
        share(batch, 1 - core).wait_recv()
        for j, total in products(1 - core, batch):
            acc[j, :rows] += total

    for j in range(Y // 2):
        pair = jnp.concatenate([acc[2 * j], acc[2 * j + 1]], axis=0)
        pair = jnp.transpose(pair).astype(bf16)
        for t in range(Y):
            sent[t, :, j * QBLOCK : (j + 1) * QBLOCK] = pair[t * 16 : (t + 1) * 16]
    copies = []
    for k in order:
        to = (y + k) % Y
        copies.append(remote(sent.at[to], came.at[y], s1.at[k], r1.at[k], column[k - 1]))
        copies[-1].start()
    came[pl.ds(y, 1)] = sent[pl.ds(y, 1)]
    for copy in copies:
        copy.wait()
    total = came[0].astype(f32)
    for j in range(1, Y):
        total += came[j].astype(f32)
    for i in range(2):
        for q in range(4):
            part = total[i * 8 : (i + 1) * 8, q * 128 : (q + 1) * 128]
            for j in range(XZ):
                turned[j % ZH, j // ZH, i * 4 + q : i * 4 + q + 1, :] = part[j : j + 1]
    cross = remote(turned.at[1 - zh], both.at[zh], s2.at[0], r2.at[0], near[0])
    cross.start()
    both[pl.ds(zh, 1)] = turned[pl.ds(zh, 1)]
    cross.wait()
    copies = []
    for k in range(1, X):
        src = both.at[:, (x + k) % X]
        copies.append(remote(src, out_ref.at[:, x], s2.at[k], r2.at[k], near[k]))
        copies[-1].start()
    for i in range(ZH):
        out_ref[i, pl.ds(x, 1)] = both[i, pl.ds(x, 1)]
    for copy in copies:
        copy.wait()

    for batch in range(batches):
        for k in order:
            relay(batch, k).wait_send()
        share(batch, core).wait_send()
    adding.finish()


def adam_kernel(g_ref, p_ref, one_ref, two_ref, newp_ref, newone_ref, newtwo_ref):
    for b in range(g_ref.shape[3] // QBLOCK):
        cut = slice(b * QBLOCK, (b + 1) * QBLOCK)
        one, two, updated = adam(
            g_ref[0, 0, :, cut].astype(f32), p_ref[:, cut].astype(f32), one_ref[:, cut], two_ref[:, cut]
        )
        newone_ref[:, cut] = one
        newtwo_ref[:, cut] = two
        newp_ref[:, cut] = updated.astype(bf16)


def body(grad_parts, master, moment_one, moment_two, gate_up, tokens, expert_ids, gate_vals):
    shape = jax.ShapeDtypeStruct
    rows, columns = master.shape
    width = tokens.shape[1]
    full = width + QBLOCK
    half = columns // 2
    size = half // CHUNKS
    tok = Y * 16
    sem = DMA((CHUNKS,))
    chunk = pltpu.VMEM((CHUNKS, rows, size), bf16)
    total, done = pl.pallas_call(
        main_kernel,
        out_shape=(
            shape((2, CHUNKS, rows, size), bf16),
            shape((ZH, X, 8, 128), f32),
        ),
        in_specs=[VMEM] * 3 + [ANY] * 5,
        out_specs=(VMEM, VMEM),
        scratch_shapes=[
            pltpu.VMEM((2, full), bf16),
            pltpu.VMEM((XZ, 2, full), bf16),
            pltpu.VMEM((16, full), f32),
            pltpu.VMEM((Y, 16, full), bf16),
            pltpu.VMEM((2 * width, QBLOCK), bf16),
            pltpu.VMEM((512, QBLOCK), f32),
            pltpu.VMEM((width, 2 * QBLOCK), bf16),
            pltpu.VMEM((rows, half), bf16),
            pltpu.VMEM((rows, half), f32),
            pltpu.VMEM((rows, half), f32),
            pltpu.VMEM((2, Y, rows, 3 * QBLOCK), bf16),
            pltpu.VMEM((2, 2, Y, rows, 3 * QBLOCK), bf16),
            pltpu.VMEM((QBLOCK, tok), bf16),
            pltpu.VMEM((XZ, QBLOCK, tok), bf16),
            pltpu.VMEM((Y, 64, tok), f32),
            pltpu.VMEM((Y, 16, 512), bf16),
            pltpu.VMEM((Y, 16, 512), bf16),
            pltpu.VMEM((ZH, X, 8, 128), f32),
            pltpu.VMEM((ZH, X, 8, 128), f32),
            DMA((4,)),
        ]
        + GATHER_SEMS
        + RING_SEMS
        + GATHER_SEMS
        + [DMA((2, 8)), DMA((2, 8)), DMA((2,)), DMA((2,)), DMA((8,)), DMA((8,)), DMA((4,)), DMA((4,))]
        + [chunk, chunk, pltpu.VMEM((2, CHUNKS, rows, size), bf16), chunk]
        + [sem, sem, sem, sem, DMA((2, CHUNKS)), sem, sem, sem, sem],
        compiler_params=pltpu.CompilerParams(
            collective_id=0, has_side_effects=True, vmem_limit_bytes=48 * 2**20
        ),
    )(
        tokens, expert_ids, gate_vals, grad_parts[0], master, moment_one, moment_two,
        gate_up.reshape(2 * width, QBLOCK),
    )

    spec = pl.BlockSpec((rows, size), lambda e: (0, e))
    new_master, new_one, new_two = pl.pallas_call(
        adam_kernel,
        grid=(2 * CHUNKS,),
        out_shape=(
            shape((rows, columns), bf16),
            shape((rows, columns), f32),
            shape((rows, columns), f32),
        ),
        in_specs=[pl.BlockSpec((1, 1, rows, size), lambda e: (e // CHUNKS, e % CHUNKS, 0, 0)), spec, spec, spec],
        out_specs=(spec, spec, spec),
        compiler_params=pltpu.CompilerParams(vmem_limit_bytes=40 * 2**20),
    )(total, master, moment_one, moment_two)

    done = done.reshape(ZH, X, 2, Y, 64)[..., :rows].transpose(2, 1, 0, 3, 4).reshape(2, width)
    return new_master, new_one, new_two, done.astype(bf16)


def solution(mesh):
    in_specs = (
        P("wide", "narrow", None),
        P("narrow", None),
        P("narrow", None),
        P("narrow", None),
        P(None, None, "narrow"),
        P(("wide", "narrow"), None),
        P(("wide", "narrow"), None),
        P(("wide", "narrow"), None),
    )
    out_specs = (
        P("narrow", None),
        P("narrow", None),
        P("narrow", None),
        P(("wide", "narrow"), None),
    )
    return jax.shard_map(body, mesh=mesh, in_specs=in_specs, out_specs=out_specs, check_vma=False)
```

```python
import jax
import jax.numpy as jnp
from jax import lax
from jax.experimental import pallas as pl
from jax.experimental.pallas import tpu as pltpu
from jax.sharding import PartitionSpec as P

EXPERTS = 8
QBLOCK = 128
X, ZH, Y = 4, 2, 8
XZ = X * ZH
ZL = 6
CHUNKS = 4

beta_first = 0.9
beta_second = 0.95
learn_rate = 0.003
adam_eps = 1e-08
quant_limit = 448.0
amax_eps = 1e-06
bias_first = 1.0 - 0.9**10
bias_second = 1.0 - 0.95**10

VMEM = pl.BlockSpec(memory_space=pltpu.VMEM)
ANY = pl.BlockSpec(memory_space=pl.ANY)
DMA = pltpu.SemaphoreType.DMA
f32 = jnp.float32
bf16 = jnp.bfloat16


def at_wide(index):
    return {"wide": index}


def remote(src, dst, send, recv, where):
    return pltpu.make_async_remote_copy(
        src_ref=src,
        dst_ref=dst,
        send_sem=send,
        recv_sem=recv,
        device_id=where,
        device_id_type=pl.DeviceIdType.MESH,
    )


def signal(where):
    pl.semaphore_signal(
        pltpu.get_barrier_semaphore(), inc=1, device_id=where, device_id_type=pl.DeviceIdType.MESH
    )


def place():
    n = lax.axis_index("narrow")
    return n // (ZH * Y), (n // Y) % ZH, n % Y


def device(x, zh, y):
    w = lax.axis_index("wide")
    own = (lax.axis_index("narrow") // Y) % ZH
    mirrored = (ZL - 1 - w // 2) * 2 + w % 2
    return {"wide": jnp.where(zh == own, w, mirrored), "narrow": (x * ZH + zh) * Y + y}


GATHER_SEMS = [DMA((9,))]
RING_SEMS = [DMA((4,)), DMA((4,)), DMA((4,)), DMA((4,))]


class Gather:
    def __init__(self, own, landing, sems):
        x, zh, y = place()
        me = x * ZH + zh
        self.local = pltpu.make_async_copy(own, landing.at[me], sems.at[8])
        self.cross = remote(own, landing.at[me], sems.at[0], sems.at[1], device(x, 1 - zh, y))
        pair = landing.at[pl.ds(x * ZH, ZH)]
        self.along = [
            remote(pair, pair, sems.at[1 + k], sems.at[4 + k], device((x + k) % X, zh, y))
            for k in range(1, X)
        ]

    def start(self):
        self.cross.start()
        self.local.start()

    def turn(self):
        self.local.wait()
        self.cross.wait()
        for copy in self.along:
            copy.start()

    def finish(self):
        for copy in self.along:
            copy.wait()


class Ring:
    def __init__(self, blocks, cut, right_send, right_recv, left_send, left_recv):
        x, zh, y = place()
        right, left = device(x, zh, (y + 1) % Y), device(x, zh, (y + Y - 1) % Y)
        self.steps = []
        for s in range(Y // 2):
            first, second = blocks.at[(y + Y - s) % Y], blocks.at[(y + s) % Y]
            if s == Y // 2 - 1:
                first, second = first.at[:, :cut], second.at[:, cut:]
            self.steps.append(
                (
                    remote(first, first, right_send.at[s], right_recv.at[s], right),
                    remote(second, second, left_send.at[s], left_recv.at[s], left),
                )
            )

    def start(self, s):
        for copy in self.steps[s]:
            copy.start()

    def wait(self, s):
        for copy in self.steps[s]:
            copy.wait()


class Sum:
    def __init__(self, g_ref, out_ref, own, pre, land, part, ld, ps, pr, is_, ir, os_, or_, cs, cr):
        w = lax.axis_index("wide")
        zl, core = w // 2, w % 2
        half = g_ref.shape[1] // 2
        size = half // CHUNKS
        low = zl < ZL // 2
        edge = (zl == 0) | (zl == ZL - 1)
        mid = (zl == ZL // 2 - 1) | (zl == ZL // 2)
        inward = at_wide(jnp.where(low, w + 2, w - 2))
        outward = at_wide(jnp.where(edge, w, jnp.where(low, w - 2, w + 2)))
        other = at_wide(w + 1 - 2 * core)
        self.edge, self.mid, self.inner = edge, mid, jnp.logical_not(edge | mid)
        self.core, self.inward, self.outward, self.other = core, inward, outward, other
        self.out_ref, self.own, self.pre, self.land, self.part = out_ref, own, pre, land, part

        def span(core_of, k):
            return pl.ds(pl.multiple_of(core_of * half + k * size, size), size)

        def load(k):
            return pltpu.make_async_copy(g_ref.at[:, span(core, k)], own.at[k], ld.at[k])

        def pre_copy(k):
            return remote(g_ref.at[:, span(1 - core, k)], pre.at[k], ps.at[k], pr.at[k], other)

        def in_copy(k, slot):
            return remote(part.at[k], land.at[slot, k], is_.at[k], ir.at[slot, k], inward)

        def out_copy(k):
            cut = out_ref.at[core, k]
            return remote(cut, cut, os_.at[k], or_.at[k], outward)

        def core_copy(k, which):
            cut = out_ref.at[which, k]
            return remote(cut, cut, cs.at[k], cr.at[k], other)

        self.load, self.pre_copy, self.in_copy, self.out_copy, self.core_copy = (
            load, pre_copy, in_copy, out_copy, core_copy,
        )

    def greet(self):
        signal(self.inward)
        signal(self.other)
        pl.when(jnp.logical_not(self.edge))(lambda: signal(self.outward))
        return jnp.where(self.edge, 2, 3)

    def start(self):
        for k in range(CHUNKS):
            self.pre_copy(k).start()

    def edge_in(self):
        @pl.when(self.edge)
        def _():
            for k in range(CHUNKS):
                self.load(k).wait()
                self.pre_copy(k).wait_recv()
                self.part[k] = (self.own[k].astype(f32) + self.pre[k].astype(f32)).astype(bf16)
                self.in_copy(k, 0).start()

    def pass_in(self, role, slot, k):
        @pl.when(role)
        def _():
            self.load(k).wait()
            self.pre_copy(k).wait_recv()
            total = self.own[k].astype(f32) + self.pre[k].astype(f32)
            self.in_copy(k, 0).wait_recv()
            self.part[k] = (total + self.land[0, k].astype(f32)).astype(bf16)
            self.in_copy(k, slot).start()

    def inner_in(self, k):
        self.pass_in(self.inner, 0, k)

    def mid_in(self, k):
        self.pass_in(self.mid, 1, k)

    def middle(self, k):
        @pl.when(self.mid)
        def _():
            self.in_copy(k, 1).wait_recv()
            total = self.part[k].astype(f32) + self.land[1, k].astype(f32)
            self.out_ref[pl.ds(self.core, 1), k] = total.astype(bf16)[None]
            self.out_copy(k).start()
            self.core_copy(k, self.core).start()

    def inner_out(self, k):
        @pl.when(self.inner)
        def _():
            self.out_copy(k).wait_recv()
            self.out_copy(k).start()
            self.core_copy(k, self.core).start()

    def edge_out(self, k):
        @pl.when(self.edge)
        def _():
            self.out_copy(k).wait_recv()
            self.core_copy(k, self.core).start()

    def finish(self):
        for k in range(CHUNKS):
            self.core_copy(k, 1 - self.core).wait_recv()
            self.pre_copy(k).wait_send()
            self.in_copy(k, 0).wait_send()
            self.core_copy(k, self.core).wait_send()

        @pl.when(jnp.logical_not(self.edge))
        def _():
            for k in range(CHUNKS):
                self.out_copy(k).wait_send()


def adam(grad, master, moment_one, moment_two):
    one = beta_first * moment_one + (1.0 - beta_first) * grad
    two = beta_second * moment_two + (1.0 - beta_second) * grad * grad
    step_dir = one * (1.0 / bias_first) / (jnp.sqrt(two * (1.0 / bias_second)) + adam_eps)
    return one, two, master - learn_rate * step_dir


def main_kernel(
    tok_any, ids_any, gate_any, g_ref, p_ref, one_ref, two_ref, w_ref,
    sum_ref, out_ref,
    tok_ref, ids_ref, gate_ref, own, landing, wide_rows, gathered, w_raw, w_tmp, w_both,
    p_half, one_half, two_half, q_first, q_last, rows_first, rows_last,
    hid_own, hid_all, acc, sent, came, turned,
    ld, sems, rs, rr, ls, lr, hsems, ys, yr, cs, cr, s1, r1, s2, r2, *rest
):
    x, zh, y = place()
    w = lax.axis_index("wide")
    core = w % 2
    other = at_wide(w + 1 - 2 * core)
    expert = x * ZH + zh
    rows, columns = p_ref.shape
    half = columns // 2
    width = tok_any.shape[1]
    per = EXPERTS // 2
    batches, fit = 2, per // 2
    q_send, rows_all = (q_first, q_last), (rows_first, rows_last)
    adding = Sum(g_ref, sum_ref, *rest)

    count = adding.greet()
    column = [device(x, zh, (y + k) % Y) for k in range(1, Y)]
    plane = []
    for k in range(1, XZ):
        to = (expert + k) % XZ
        plane.append(device(to // ZH, to % ZH, y))
    for where in column + plane:
        signal(where)

    small_loads = [
        pltpu.make_async_copy(tok_any, tok_ref, ld.at[4]),
        pltpu.make_async_copy(ids_any, ids_ref, ld.at[5]),
        pltpu.make_async_copy(gate_any, gate_ref, ld.at[6]),
    ]
    for copy in small_loads:
        copy.start()
    span = pl.ds(pl.multiple_of(core * half, half), half)
    w_load = pltpu.make_async_copy(w_ref, w_raw, ld.at[0])
    state_loads = [
        pltpu.make_async_copy(p_ref.at[:, span], p_half, ld.at[1]),
        pltpu.make_async_copy(one_ref.at[:, span], one_half, ld.at[2]),
        pltpu.make_async_copy(two_ref.at[:, span], two_half, ld.at[3]),
    ]
    for k in range(CHUNKS):
        adding.load(k).start()
    w_load.start()
    for copy in state_loads:
        copy.start()

    for copy in small_loads:
        copy.wait()
    own[:, :width] = tok_ref[...]
    lane = lax.broadcasted_iota(jnp.int32, (2, QBLOCK), 1)
    weights = jnp.zeros((2, QBLOCK), f32)
    for k in range(ids_ref.shape[1]):
        gate = gate_ref[:, k : k + 1].astype(f32)
        weights += jnp.where(ids_ref[:, k : k + 1] == lane, gate, 0.0)
    own[:, width:] = weights.astype(bf16)
    pl.semaphore_wait(pltpu.get_barrier_semaphore(), count + len(column) + len(plane))

    gather = Gather(own, landing, sems)
    ring = Ring(gathered, own.shape[1] // 256 * 128, rs, rr, ls, lr)
    gather.start()
    adding.start()
    adding.edge_in()

    w_load.wait()
    piece = w_tmp.shape[0]

    def split(i, carry):
        w_tmp[...] = w_raw[pl.ds(pl.multiple_of(i * piece, piece), piece), :].astype(f32)
        to = pl.ds(pl.multiple_of(i * (piece // 2), piece // 2), piece // 2)
        w_both[to, :QBLOCK] = w_tmp[pl.ds(0, piece // 2, stride=2), :].astype(bf16)
        w_both[to, QBLOCK:] = w_tmp[pl.ds(1, piece // 2, stride=2), :].astype(bf16)
        return carry

    lax.fori_loop(0, w_raw.shape[0] // piece, split, 0)

    gather.turn()
    adding.inner_in(0)
    gather.finish()
    for j in range(XZ):
        for i in range(2):
            wide_rows[i * XZ + j : i * XZ + j + 1, :] = landing[j, i : i + 1, :].astype(f32)
    gathered[pl.ds(y, 1)] = wide_rows[...].astype(bf16)[None]
    ring.start(0)
    for copy in state_loads:
        copy.wait()

    def quantize(k):
        for b in range(Y):
            cut = slice(k * Y * QBLOCK + b * QBLOCK, k * Y * QBLOCK + (b + 1) * QBLOCK)
            grad = sum_ref[core, k, :, b * QBLOCK : (b + 1) * QBLOCK].astype(f32)
            _, _, updated = adam(grad, p_half[:, cut].astype(f32), one_half[:, cut], two_half[:, cut])
            amax = jnp.max(jnp.abs(updated), axis=1, keepdims=True)
            scale = ((amax + amax_eps) / quant_limit).astype(bf16)
            quanta = (updated * (1.0 / scale.astype(f32))).astype(bf16)
            spot = k % fit
            q_send[k // fit][b, :, spot * QBLOCK : (spot + 1) * QBLOCK] = quanta
            q_send[1][b, :, fit * QBLOCK + k : fit * QBLOCK + k + 1] = scale

    order = [1, 7, 2, 6, 3, 5, 4]

    def relay(batch, k):
        return remote(
            q_send[batch].at[(y + k) % Y], rows_all[batch].at[core, y],
            ys.at[batch, k], yr.at[batch, k], column[k - 1],
        )

    def mine(batch):
        return pltpu.make_async_copy(
            q_send[batch].at[y], rows_all[batch].at[core, y], ys.at[batch, 0]
        )

    def relay_start(batch):
        for k in order:
            relay(batch, k).start()
        mine(batch).start()

    def share(batch, which):
        part = rows_all[batch].at[which]
        return remote(part, part, cs.at[batch], cr.at[batch], other)

    def relay_finish(batch):
        mine(batch).wait()
        for k in order:
            relay(batch, k).wait_recv()
        share(batch, core).start()

    adding.inner_in(1)
    adding.inner_in(2)
    adding.mid_in(0)
    adding.mid_in(1)
    ring.wait(0)
    ring.start(1)
    adding.inner_in(3)
    adding.mid_in(2)
    adding.middle(0)
    adding.middle(1)
    adding.mid_in(3)
    ring.wait(1)
    ring.start(2)
    adding.middle(2)
    adding.middle(3)
    adding.inner_out(0)
    adding.inner_out(1)
    ring.wait(2)
    ring.start(3)
    adding.inner_out(2)
    adding.inner_out(3)
    adding.edge_out(0)
    quantize(0)
    adding.edge_out(1)
    quantize(1)
    relay_start(0)
    ring.wait(3)

    tokens = gathered.reshape(Y * 16, own.shape[1])
    proj = jnp.dot(tokens[:, :width], w_both[...], preferred_element_type=f32)
    weight = tokens[:, width:].astype(f32)
    lanes = lax.broadcasted_iota(jnp.int32, weight.shape, 1)
    weight = jnp.sum(jnp.where(lanes == expert, weight, 0.0), axis=1, keepdims=True)
    gate = proj[:, :QBLOCK]
    hidden = weight * (gate * jax.nn.sigmoid(gate)) * proj[:, QBLOCK:]
    hid_own[...] = jnp.transpose(hidden).astype(bf16)
    hid_gather = Gather(hid_own, hid_all, hsems)
    hid_gather.start()
    adding.edge_out(2)
    quantize(2)
    adding.edge_out(3)
    quantize(3)
    relay_start(1)
    relay_finish(0)
    hid_gather.turn()
    relay_finish(1)
    hid_gather.finish()

    def products(which, j):
        total = None
        for e in range(per):
            spot = e % fit
            quanta = rows_all[e // fit][which, j, :, spot * QBLOCK : (spot + 1) * QBLOCK]
            scale = rows_all[1][which, j, :, fit * QBLOCK + e : fit * QBLOCK + e + 1].astype(f32)
            term = scale * jnp.dot(quanta, hid_all[which * per + e], preferred_element_type=f32)
            total = term if total is None else total + term
        return total

    for j in range(Y):
        acc[j, :rows] = products(core, j)
        acc[j, rows:] = jnp.zeros_like(acc[j, rows:])
    for batch in range(batches):
        share(batch, 1 - core).wait_recv()
    for j in range(Y):
        acc[j, :rows] += products(1 - core, j)

    for j in range(Y // 2):
        pair = jnp.concatenate([acc[2 * j], acc[2 * j + 1]], axis=0)
        pair = jnp.transpose(pair).astype(bf16)
        for t in range(Y):
            sent[t, :, j * QBLOCK : (j + 1) * QBLOCK] = pair[t * 16 : (t + 1) * 16]
    copies = []
    for k in order:
        to = (y + k) % Y
        copies.append(remote(sent.at[to], came.at[y], s1.at[k], r1.at[k], column[k - 1]))
        copies[-1].start()
    came[pl.ds(y, 1)] = sent[pl.ds(y, 1)]
    for copy in copies:
        copy.wait()
    total = came[0].astype(f32)
    for j in range(1, Y):
        total += came[j].astype(f32)
    for i in range(2):
        for q in range(4):
            part = total[i * 8 : (i + 1) * 8, q * 128 : (q + 1) * 128]
            turned[:, i * 4 + q, :] = part
    copies = []
    for k in range(1, XZ):
        to = (expert + k) % XZ
        copies.append(remote(turned.at[to], out_ref.at[expert], s2.at[k], r2.at[k], plane[k - 1]))
        copies[-1].start()
    out_ref[pl.ds(expert, 1)] = turned[pl.ds(expert, 1)]
    for copy in copies:
        copy.wait()

    for batch in range(batches):
        for k in order:
            relay(batch, k).wait_send()
        share(batch, core).wait_send()
    adding.finish()


def adam_kernel(g_ref, p_ref, one_ref, two_ref, newp_ref, newone_ref, newtwo_ref):
    for b in range(g_ref.shape[3] // QBLOCK):
        cut = slice(b * QBLOCK, (b + 1) * QBLOCK)
        one, two, updated = adam(
            g_ref[0, 0, :, cut].astype(f32), p_ref[:, cut].astype(f32), one_ref[:, cut], two_ref[:, cut]
        )
        newone_ref[:, cut] = one
        newtwo_ref[:, cut] = two
        newp_ref[:, cut] = updated.astype(bf16)


def body(grad_parts, master, moment_one, moment_two, gate_up, tokens, expert_ids, gate_vals):
    shape = jax.ShapeDtypeStruct
    rows, columns = master.shape
    width = tokens.shape[1]
    full = width + QBLOCK
    half = columns // 2
    size = half // CHUNKS
    tok = Y * 16
    sem = DMA((CHUNKS,))
    chunk = pltpu.VMEM((CHUNKS, rows, size), bf16)
    total, done = pl.pallas_call(
        main_kernel,
        out_shape=(
            shape((2, CHUNKS, rows, size), bf16),
            shape((XZ, 8, 128), f32),
        ),
        in_specs=[ANY] * 8,
        out_specs=(VMEM, VMEM),
        scratch_shapes=[
            pltpu.VMEM(tokens.shape, bf16),
            pltpu.VMEM(expert_ids.shape, jnp.int32),
            pltpu.VMEM(gate_vals.shape, bf16),
            pltpu.VMEM((2, full), bf16),
            pltpu.VMEM((XZ, 2, full), bf16),
            pltpu.VMEM((16, full), f32),
            pltpu.VMEM((Y, 16, full), bf16),
            pltpu.VMEM((2 * width, QBLOCK), bf16),
            pltpu.VMEM((512, QBLOCK), f32),
            pltpu.VMEM((width, 2 * QBLOCK), bf16),
            pltpu.VMEM((rows, half), bf16),
            pltpu.VMEM((rows, half), f32),
            pltpu.VMEM((rows, half), f32),
            pltpu.VMEM((Y, rows, 2 * QBLOCK), bf16),
            pltpu.VMEM((Y, rows, 3 * QBLOCK), bf16),
            pltpu.VMEM((2, Y, rows, 2 * QBLOCK), bf16),
            pltpu.VMEM((2, Y, rows, 3 * QBLOCK), bf16),
            pltpu.VMEM((QBLOCK, tok), bf16),
            pltpu.VMEM((XZ, QBLOCK, tok), bf16),
            pltpu.VMEM((Y, 64, tok), f32),
            pltpu.VMEM((Y, 16, 512), bf16),
            pltpu.VMEM((Y, 16, 512), bf16),
            pltpu.VMEM((XZ, 8, 128), f32),
            DMA((7,)),
        ]
        + GATHER_SEMS
        + RING_SEMS
        + GATHER_SEMS
        + [DMA((2, 8)), DMA((2, 8)), DMA((2,)), DMA((2,)), DMA((8,)), DMA((8,)), DMA((8,)), DMA((8,))]
        + [chunk, chunk, pltpu.VMEM((2, CHUNKS, rows, size), bf16), chunk]
        + [sem, sem, sem, sem, DMA((2, CHUNKS)), sem, sem, sem, sem],
        compiler_params=pltpu.CompilerParams(
            collective_id=0, has_side_effects=True, vmem_limit_bytes=62 * 2**20
        ),
    )(
        tokens, expert_ids, gate_vals, grad_parts[0], master, moment_one, moment_two,
        gate_up.reshape(2 * width, QBLOCK),
    )

    spec = pl.BlockSpec((rows, size), lambda e: (0, e))
    new_master, new_one, new_two = pl.pallas_call(
        adam_kernel,
        grid=(2 * CHUNKS,),
        out_shape=(
            shape((rows, columns), bf16),
            shape((rows, columns), f32),
            shape((rows, columns), f32),
        ),
        in_specs=[pl.BlockSpec((1, 1, rows, size), lambda e: (e // CHUNKS, e % CHUNKS, 0, 0)), spec, spec, spec],
        out_specs=(spec, spec, spec),
        compiler_params=pltpu.CompilerParams(vmem_limit_bytes=62 * 2**20),
    )(total, master, moment_one, moment_two)

    done = done.reshape(XZ, 2, Y, 64)[..., :rows].transpose(1, 0, 2, 3).reshape(2, width)
    return new_master, new_one, new_two, done.astype(bf16)


def solution(mesh):
    in_specs = (
        P("wide", "narrow", None),
        P("narrow", None),
        P("narrow", None),
        P("narrow", None),
        P(None, None, "narrow"),
        P(("wide", "narrow"), None),
        P(("wide", "narrow"), None),
        P(("wide", "narrow"), None),
    )
    out_specs = (
        P("narrow", None),
        P("narrow", None),
        P("narrow", None),
        P(("wide", "narrow"), None),
    )
    return jax.shard_map(body, mesh=mesh, in_specs=in_specs, out_specs=out_specs, check_vma=False)
```

```python
import jax
import jax.numpy as jnp
from jax import lax
from jax.experimental import pallas as pl
from jax.experimental.pallas import tpu as pltpu
from jax.sharding import PartitionSpec as P

EXPERTS = 8
QBLOCK = 128
X, ZH, Y = 4, 2, 8
XZ = X * ZH
ZL = 6
CHUNKS = 4

beta_first = 0.9
beta_second = 0.95
learn_rate = 0.003
adam_eps = 1e-08
quant_limit = 448.0
amax_eps = 1e-06
bias_first = 1.0 - 0.9**10
bias_second = 1.0 - 0.95**10

VMEM = pl.BlockSpec(memory_space=pltpu.VMEM)
HBM = pl.BlockSpec(memory_space=pltpu.HBM)
DMA = pltpu.SemaphoreType.DMA
f32 = jnp.float32
bf16 = jnp.bfloat16


def at_wide(index):
    return {"wide": index}


def remote(src, dst, send, recv, where):
    return pltpu.make_async_remote_copy(
        src_ref=src,
        dst_ref=dst,
        send_sem=send,
        recv_sem=recv,
        device_id=where,
        device_id_type=pl.DeviceIdType.MESH,
    )


def signal(where):
    pl.semaphore_signal(
        pltpu.get_barrier_semaphore(), inc=1, device_id=where, device_id_type=pl.DeviceIdType.MESH
    )


def place():
    n = lax.axis_index("narrow")
    return n // (ZH * Y), (n // Y) % ZH, n % Y


def device(x, zh, y):
    w = lax.axis_index("wide")
    own = (lax.axis_index("narrow") // Y) % ZH
    mirrored = (ZL - 1 - w // 2) * 2 + w % 2
    return {"wide": jnp.where(zh == own, w, mirrored), "narrow": (x * ZH + zh) * Y + y}


GATHER_SEMS = [DMA((9,))]
RING_SEMS = [DMA((4,)), DMA((4,)), DMA((4,)), DMA((4,))]


class Gather:
    def __init__(self, own, landing, sems):
        x, zh, y = place()
        me = x * ZH + zh
        self.local = pltpu.make_async_copy(own, landing.at[me], sems.at[8])
        self.cross = remote(own, landing.at[me], sems.at[0], sems.at[1], device(x, 1 - zh, y))
        pair = landing.at[pl.ds(x * ZH, ZH)]
        self.along = [
            remote(pair, pair, sems.at[1 + k], sems.at[4 + k], device((x + k) % X, zh, y))
            for k in range(1, X)
        ]

    def start(self):
        self.cross.start()
        self.local.start()

    def turn(self):
        self.local.wait()
        self.cross.wait()
        for copy in self.along:
            copy.start()

    def finish(self):
        for copy in self.along:
            copy.wait()


class Ring:
    def __init__(self, blocks, cut, right_send, right_recv, left_send, left_recv):
        x, zh, y = place()
        right, left = device(x, zh, (y + 1) % Y), device(x, zh, (y + Y - 1) % Y)
        self.steps = []
        for s in range(Y // 2):
            first, second = blocks.at[(y + Y - s) % Y], blocks.at[(y + s) % Y]
            if s == Y // 2 - 1:
                first, second = first.at[:, :cut], second.at[:, cut:]
            self.steps.append(
                (
                    remote(first, first, right_send.at[s], right_recv.at[s], right),
                    remote(second, second, left_send.at[s], left_recv.at[s], left),
                )
            )

    def start(self, s):
        for copy in self.steps[s]:
            copy.start()

    def wait(self, s):
        for copy in self.steps[s]:
            copy.wait()


class Sum:
    def __init__(self, g_ref, out_ref, own, pre, land, part, ld, ps, pr, is_, ir, os_, or_, cs, cr):
        w = lax.axis_index("wide")
        zl, core = w // 2, w % 2
        half = g_ref.shape[1] // 2
        size = half // CHUNKS
        low = zl < ZL // 2
        edge = (zl == 0) | (zl == ZL - 1)
        mid = (zl == ZL // 2 - 1) | (zl == ZL // 2)
        inward = at_wide(jnp.where(low, w + 2, w - 2))
        outward = at_wide(jnp.where(edge, w, jnp.where(low, w - 2, w + 2)))
        other = at_wide(w + 1 - 2 * core)
        self.edge, self.mid, self.inner = edge, mid, jnp.logical_not(edge | mid)
        self.core, self.inward, self.outward, self.other = core, inward, outward, other
        self.out_ref, self.own, self.pre, self.land, self.part = out_ref, own, pre, land, part

        def span(core_of, k):
            return pl.ds(pl.multiple_of(core_of * half + k * size, size), size)

        def load(k):
            return pltpu.make_async_copy(g_ref.at[:, span(core, k)], own.at[k], ld.at[k])

        def pre_copy(k):
            return remote(g_ref.at[:, span(1 - core, k)], pre.at[k], ps.at[k], pr.at[k], other)

        def in_copy(k, slot):
            return remote(part.at[k], land.at[slot, k], is_.at[k], ir.at[slot, k], inward)

        def out_copy(k):
            cut = out_ref.at[core, k]
            return remote(cut, cut, os_.at[k], or_.at[k], outward)

        def core_copy(k, which):
            cut = out_ref.at[which, k]
            return remote(cut, cut, cs.at[k], cr.at[k], other)

        self.load, self.pre_copy, self.in_copy, self.out_copy, self.core_copy = (
            load, pre_copy, in_copy, out_copy, core_copy,
        )

    def greet(self):
        signal(self.inward)
        signal(self.other)
        pl.when(jnp.logical_not(self.edge))(lambda: signal(self.outward))
        return jnp.where(self.edge, 2, 3)

    def start(self):
        for k in range(CHUNKS):
            self.pre_copy(k).start()

    def edge_in(self):
        @pl.when(self.edge)
        def _():
            for k in range(CHUNKS):
                self.load(k).wait()
                self.pre_copy(k).wait_recv()
                self.part[k] = (self.own[k].astype(f32) + self.pre[k].astype(f32)).astype(bf16)
                self.in_copy(k, 0).start()

    def pass_in(self, role, slot, k):
        @pl.when(role)
        def _():
            self.load(k).wait()
            self.pre_copy(k).wait_recv()
            total = self.own[k].astype(f32) + self.pre[k].astype(f32)
            self.in_copy(k, 0).wait_recv()
            self.part[k] = (total + self.land[0, k].astype(f32)).astype(bf16)
            self.in_copy(k, slot).start()

    def inner_in(self, k):
        self.pass_in(self.inner, 0, k)

    def mid_in(self, k):
        self.pass_in(self.mid, 1, k)

    def middle(self, k):
        @pl.when(self.mid)
        def _():
            self.in_copy(k, 1).wait_recv()
            total = self.part[k].astype(f32) + self.land[1, k].astype(f32)
            self.out_ref[pl.ds(self.core, 1), k] = total.astype(bf16)[None]
            self.out_copy(k).start()
            self.core_copy(k, self.core).start()

    def inner_out(self, k):
        @pl.when(self.inner)
        def _():
            self.out_copy(k).wait_recv()
            self.out_copy(k).start()
            self.core_copy(k, self.core).start()

    def edge_out(self, k):
        @pl.when(self.edge)
        def _():
            self.out_copy(k).wait_recv()
            self.core_copy(k, self.core).start()

    def finish(self):
        for k in range(CHUNKS):
            self.pre_copy(k).wait_send()
            self.in_copy(k, 0).wait_send()
            self.core_copy(k, self.core).wait_send()

        @pl.when(jnp.logical_not(self.edge))
        def _():
            for k in range(CHUNKS):
                self.out_copy(k).wait_send()


def adam(grad, master, moment_one, moment_two):
    one = beta_first * moment_one + (1.0 - beta_first) * grad
    two = beta_second * moment_two + (1.0 - beta_second) * grad * grad
    step_dir = one * (1.0 / bias_first) / (jnp.sqrt(two * (1.0 / bias_second)) + adam_eps)
    return one, two, master - learn_rate * step_dir


def main_kernel(
    tok_any, ids_any, gate_any, g_ref, p_ref, one_ref, two_ref, w_ref,
    newp_ref, newone_ref, newtwo_ref, out_ref,
    tok_ref, ids_ref, gate_ref, own, landing, wide_rows, gathered, w_raw, w_tmp, w_both,
    sum_ref, final, q_first, q_last, rows_first, rows_last,
    hid_own, hid_all, acc, sent, came, turned,
    ld, sems, rs, rr, ls, lr, hsems, ys, yr, cs, cr, s1, r1, s2, r2, *rest
):
    x, zh, y = place()
    w = lax.axis_index("wide")
    core = w % 2
    other = at_wide(w + 1 - 2 * core)
    expert = x * ZH + zh
    rows, columns = p_ref.shape
    half = columns // 2
    width = tok_any.shape[1]
    per = EXPERTS // 2
    batches, fit = 2, per // 2
    q_send, rows_all = (q_first, q_last), (rows_first, rows_last)
    adding = Sum(g_ref, sum_ref, *rest)

    count = adding.greet()
    column = [device(x, zh, (y + k) % Y) for k in range(1, Y)]
    plane = []
    for k in range(1, XZ):
        to = (expert + k) % XZ
        plane.append(device(to // ZH, to % ZH, y))
    for where in column + plane:
        signal(where)

    small_loads = [
        pltpu.make_async_copy(tok_any, tok_ref, ld.at[7]),
        pltpu.make_async_copy(ids_any, ids_ref, ld.at[8]),
        pltpu.make_async_copy(gate_any, gate_ref, ld.at[9]),
    ]
    for copy in small_loads:
        copy.start()
    w_load = pltpu.make_async_copy(w_ref, w_raw, ld.at[0])
    state_loads = []
    for i, which in enumerate((core, 1 - core)):
        span = pl.ds(pl.multiple_of(which * half, half), half)
        for n, (src, dst) in enumerate(
            ((p_ref, newp_ref), (one_ref, newone_ref), (two_ref, newtwo_ref))
        ):
            state_loads.append(
                pltpu.make_async_copy(src.at[:, span], dst.at[:, span], ld.at[1 + i * 3 + n])
            )
    for k in range(CHUNKS):
        adding.load(k).start()
    w_load.start()
    for copy in state_loads:
        copy.start()

    for copy in small_loads:
        copy.wait()
    own[:, :width] = tok_ref[...]
    lane = lax.broadcasted_iota(jnp.int32, (2, QBLOCK), 1)
    weights = jnp.zeros((2, QBLOCK), f32)
    for k in range(ids_ref.shape[1]):
        gate = gate_ref[:, k : k + 1].astype(f32)
        weights += jnp.where(ids_ref[:, k : k + 1] == lane, gate, 0.0)
    own[:, width:] = weights.astype(bf16)
    pl.semaphore_wait(pltpu.get_barrier_semaphore(), count + len(column) + len(plane))

    gather = Gather(own, landing, sems)
    ring = Ring(gathered, own.shape[1] // 256 * 128, rs, rr, ls, lr)
    gather.start()
    adding.start()
    adding.edge_in()

    w_load.wait()
    piece = w_tmp.shape[0]

    def split(i, carry):
        w_tmp[...] = w_raw[pl.ds(pl.multiple_of(i * piece, piece), piece), :].astype(f32)
        to = pl.ds(pl.multiple_of(i * (piece // 2), piece // 2), piece // 2)
        w_both[to, :QBLOCK] = w_tmp[pl.ds(0, piece // 2, stride=2), :].astype(bf16)
        w_both[to, QBLOCK:] = w_tmp[pl.ds(1, piece // 2, stride=2), :].astype(bf16)
        return carry

    lax.fori_loop(0, w_raw.shape[0] // piece, split, 0)

    gather.turn()
    adding.inner_in(0)
    gather.finish()
    for j in range(XZ):
        for i in range(2):
            wide_rows[i * XZ + j : i * XZ + j + 1, :] = landing[j, i : i + 1, :].astype(f32)
    gathered[pl.ds(y, 1)] = wide_rows[...].astype(bf16)[None]
    ring.start(0)
    for copy in state_loads:
        copy.wait()

    def advance(which, k, b):
        at = which * half + (k * Y + b) * QBLOCK
        cut = pl.ds(pl.multiple_of(at, QBLOCK), QBLOCK)
        one, two, updated = adam(
            sum_ref[which, k, :, b * QBLOCK : (b + 1) * QBLOCK].astype(f32),
            newp_ref[:, cut].astype(f32),
            newone_ref[:, cut],
            newtwo_ref[:, cut],
        )
        newone_ref[:, cut] = one
        newtwo_ref[:, cut] = two
        newp_ref[:, cut] = updated.astype(bf16)
        return updated

    def quantize(k):
        for b in range(Y):
            updated = advance(core, k, b)
            amax = jnp.max(jnp.abs(updated), axis=1, keepdims=True)
            scale = ((amax + amax_eps) / quant_limit).astype(bf16)
            quanta = (updated * (1.0 / scale.astype(f32))).astype(bf16)
            spot = k % fit
            q_send[k // fit][b, :, spot * QBLOCK : (spot + 1) * QBLOCK] = quanta
            q_send[1][b, :, fit * QBLOCK + k : fit * QBLOCK + k + 1] = scale

    order = [1, 7, 2, 6, 3, 5, 4]

    def relay(batch, k):
        return remote(
            q_send[batch].at[(y + k) % Y], rows_all[batch].at[core, y],
            ys.at[batch, k], yr.at[batch, k], column[k - 1],
        )

    def mine(batch):
        return pltpu.make_async_copy(
            q_send[batch].at[y], rows_all[batch].at[core, y], ys.at[batch, 0]
        )

    def relay_start(batch):
        for k in order:
            relay(batch, k).start()
        mine(batch).start()

    def share(batch, which):
        part = rows_all[batch].at[which]
        return remote(part, part, cs.at[batch], cr.at[batch], other)

    def relay_finish(batch):
        mine(batch).wait()
        for k in order:
            relay(batch, k).wait_recv()
        share(batch, core).start()

    adding.inner_in(1)
    adding.inner_in(2)
    adding.mid_in(0)
    adding.mid_in(1)
    ring.wait(0)
    ring.start(1)
    adding.inner_in(3)
    adding.mid_in(2)
    adding.middle(0)
    adding.middle(1)
    adding.mid_in(3)
    ring.wait(1)
    ring.start(2)
    adding.middle(2)
    adding.middle(3)
    adding.inner_out(0)
    adding.inner_out(1)
    ring.wait(2)
    ring.start(3)
    adding.inner_out(2)
    adding.inner_out(3)
    adding.edge_out(0)
    quantize(0)
    adding.edge_out(1)
    quantize(1)
    relay_start(0)
    ring.wait(3)

    tokens = gathered.reshape(Y * 16, own.shape[1])
    proj = jnp.dot(tokens[:, :width], w_both[...], preferred_element_type=f32)
    weight = tokens[:, width:].astype(f32)
    lanes = lax.broadcasted_iota(jnp.int32, weight.shape, 1)
    weight = jnp.sum(jnp.where(lanes == expert, weight, 0.0), axis=1, keepdims=True)
    gate = proj[:, :QBLOCK]
    hidden = weight * (gate * jax.nn.sigmoid(gate)) * proj[:, QBLOCK:]
    hid_own[...] = jnp.transpose(hidden).astype(bf16)
    hid_gather = Gather(hid_own, hid_all, hsems)
    hid_gather.start()
    adding.edge_out(2)
    quantize(2)
    adding.edge_out(3)
    quantize(3)
    relay_start(1)
    relay_finish(0)
    hid_gather.turn()
    relay_finish(1)
    hid_gather.finish()

    def products(which, j):
        total = None
        for e in range(per):
            spot = e % fit
            quanta = rows_all[e // fit][which, j, :, spot * QBLOCK : (spot + 1) * QBLOCK]
            scale = rows_all[1][which, j, :, fit * QBLOCK + e : fit * QBLOCK + e + 1].astype(f32)
            term = scale * jnp.dot(quanta, hid_all[which * per + e], preferred_element_type=f32)
            total = term if total is None else total + term
        return total

    for j in range(Y):
        acc[j, :rows] = products(core, j)
        acc[j, rows:] = jnp.zeros_like(acc[j, rows:])
    for batch in range(batches):
        share(batch, 1 - core).wait_recv()
    for j in range(Y):
        acc[j, :rows] += products(1 - core, j)

    for j in range(Y // 2):
        pair = jnp.concatenate([acc[2 * j], acc[2 * j + 1]], axis=0)
        pair = jnp.transpose(pair).astype(bf16)
        for t in range(Y):
            sent[t, :, j * QBLOCK : (j + 1) * QBLOCK] = pair[t * 16 : (t + 1) * 16]
    copies = []
    for k in order:
        to = (y + k) % Y
        copies.append(remote(sent.at[to], came.at[y], s1.at[k], r1.at[k], column[k - 1]))
        copies[-1].start()
    came[pl.ds(y, 1)] = sent[pl.ds(y, 1)]

    def other_half(k):
        adding.core_copy(k, 1 - core).wait_recv()
        for b in range(Y):
            advance(1 - core, k, b)

    other_half(0)
    other_half(1)
    for copy in copies:
        copy.wait()
    total = came[0].astype(f32)
    for j in range(1, Y):
        total += came[j].astype(f32)
    for i in range(2):
        for q in range(4):
            part = total[i * 8 : (i + 1) * 8, q * 128 : (q + 1) * 128]
            turned[:, i * 4 + q, :] = part
    copies = []
    for k in range(1, XZ):
        to = (expert + k) % XZ
        copies.append(remote(turned.at[to], final.at[expert], s2.at[k], r2.at[k], plane[k - 1]))
        copies[-1].start()
    final[pl.ds(expert, 1)] = turned[pl.ds(expert, 1)]
    other_half(2)
    other_half(3)
    for copy in copies:
        copy.wait()
    out_ref[...] = final[...].astype(bf16)

    for batch in range(batches):
        for k in order:
            relay(batch, k).wait_send()
        share(batch, core).wait_send()
    adding.finish()


def body(grad_parts, master, moment_one, moment_two, gate_up, tokens, expert_ids, gate_vals):
    shape = jax.ShapeDtypeStruct
    rows, columns = master.shape
    width = tokens.shape[1]
    full = width + QBLOCK
    size = columns // 2 // CHUNKS
    tok = Y * 16
    sem = DMA((CHUNKS,))
    chunk = pltpu.VMEM((CHUNKS, rows, size), bf16)
    new_master, new_one, new_two, done = pl.pallas_call(
        main_kernel,
        out_shape=(
            shape((rows, columns), bf16),
            shape((rows, columns), f32),
            shape((rows, columns), f32),
            shape((XZ, 8, 128), bf16),
        ),
        in_specs=[HBM] * 8,
        out_specs=(VMEM,) * 4,
        scratch_shapes=[
            pltpu.VMEM(tokens.shape, bf16),
            pltpu.VMEM(expert_ids.shape, jnp.int32),
            pltpu.VMEM(gate_vals.shape, bf16),
            pltpu.VMEM((2, full), bf16),
            pltpu.VMEM((XZ, 2, full), bf16),
            pltpu.VMEM((16, full), f32),
            pltpu.VMEM((Y, 16, full), bf16),
            pltpu.VMEM((2 * width, QBLOCK), bf16),
            pltpu.VMEM((512, QBLOCK), f32),
            pltpu.VMEM((width, 2 * QBLOCK), bf16),
            pltpu.VMEM((2, CHUNKS, rows, size), bf16),
            pltpu.VMEM((XZ, 8, 128), f32),
            pltpu.VMEM((Y, rows, 2 * QBLOCK), bf16),
            pltpu.VMEM((Y, rows, 3 * QBLOCK), bf16),
            pltpu.VMEM((2, Y, rows, 2 * QBLOCK), bf16),
            pltpu.VMEM((2, Y, rows, 3 * QBLOCK), bf16),
            pltpu.VMEM((QBLOCK, tok), bf16),
            pltpu.VMEM((XZ, QBLOCK, tok), bf16),
            pltpu.VMEM((Y, 64, tok), f32),
            pltpu.VMEM((Y, 16, 512), bf16),
            pltpu.VMEM((Y, 16, 512), bf16),
            pltpu.VMEM((XZ, 8, 128), f32),
            DMA((10,)),
        ]
        + GATHER_SEMS
        + RING_SEMS
        + GATHER_SEMS
        + [DMA((2, 8)), DMA((2, 8)), DMA((2,)), DMA((2,)), DMA((8,)), DMA((8,)), DMA((8,)), DMA((8,))]
        + [chunk, chunk, pltpu.VMEM((2, CHUNKS, rows, size), bf16), chunk]
        + [sem, sem, sem, sem, DMA((2, CHUNKS)), sem, sem, sem, sem],
        compiler_params=pltpu.CompilerParams(
            collective_id=0, has_side_effects=True, vmem_limit_bytes=36 * 2**20
        ),
    )(
        *[
            pltpu.with_memory_space_constraint(value, pltpu.HBM)
            for value in (
                tokens, expert_ids, gate_vals, grad_parts[0], master, moment_one, moment_two,
                gate_up.reshape(2 * width, QBLOCK),
            )
        ]
    )

    done = done.reshape(XZ, 2, Y, 64)[..., :rows].transpose(1, 0, 2, 3).reshape(2, width)
    return new_master, new_one, new_two, done


def solution(mesh):
    in_specs = (
        P("wide", "narrow", None),
        P("narrow", None),
        P("narrow", None),
        P("narrow", None),
        P(None, None, "narrow"),
        P(("wide", "narrow"), None),
        P(("wide", "narrow"), None),
        P(("wide", "narrow"), None),
    )
    out_specs = (
        P("narrow", None),
        P("narrow", None),
        P("narrow", None),
        P(("wide", "narrow"), None),
    )
    return jax.shard_map(body, mesh=mesh, in_specs=in_specs, out_specs=out_specs, check_vma=False)
```

```python
import jax
import jax.numpy as jnp
from jax import lax
from jax.experimental import pallas as pl
from jax.experimental.pallas import tpu as pltpu
from jax.sharding import PartitionSpec as P

EXPERTS = 8
QBLOCK = 128
X, ZH, Y = 4, 2, 8
XZ = X * ZH
ZL = 6
CHUNKS = 4

beta_first = 0.9
beta_second = 0.95
learn_rate = 0.003
adam_eps = 1e-08
quant_limit = 448.0
amax_eps = 1e-06
bias_first = 1.0 - 0.9**10
bias_second = 1.0 - 0.95**10

VMEM = pl.BlockSpec(memory_space=pltpu.VMEM)
HBM = pl.BlockSpec(memory_space=pltpu.HBM)
DMA = pltpu.SemaphoreType.DMA
f32 = jnp.float32
bf16 = jnp.bfloat16


def at_wide(index):
    return {"wide": index}


def remote(src, dst, send, recv, where):
    return pltpu.make_async_remote_copy(
        src_ref=src,
        dst_ref=dst,
        send_sem=send,
        recv_sem=recv,
        device_id=where,
        device_id_type=pl.DeviceIdType.MESH,
    )


def signal(where):
    pl.semaphore_signal(
        pltpu.get_barrier_semaphore(), inc=1, device_id=where, device_id_type=pl.DeviceIdType.MESH
    )


def place():
    n = lax.axis_index("narrow")
    return n // (ZH * Y), (n // Y) % ZH, n % Y


def device(x, zh, y):
    w = lax.axis_index("wide")
    own = (lax.axis_index("narrow") // Y) % ZH
    mirrored = (ZL - 1 - w // 2) * 2 + w % 2
    return {"wide": jnp.where(zh == own, w, mirrored), "narrow": (x * ZH + zh) * Y + y}


GATHER_SEMS = [DMA((9,))]
RING_SEMS = [DMA((4,)), DMA((4,)), DMA((4,)), DMA((4,))]


class Gather:
    def __init__(self, own, landing, sems):
        x, zh, y = place()
        me = x * ZH + zh
        self.local = pltpu.make_async_copy(own, landing.at[me], sems.at[8])
        self.cross = remote(own, landing.at[me], sems.at[0], sems.at[1], device(x, 1 - zh, y))
        pair = landing.at[pl.ds(x * ZH, ZH)]
        self.along = [
            remote(pair, pair, sems.at[1 + k], sems.at[4 + k], device((x + k) % X, zh, y))
            for k in range(1, X)
        ]

    def start(self):
        self.cross.start()
        self.local.start()

    def turn(self):
        self.local.wait()
        self.cross.wait()
        for copy in self.along:
            copy.start()

    def finish(self):
        for copy in self.along:
            copy.wait()


class Ring:
    def __init__(self, blocks, cut, right_send, right_recv, left_send, left_recv):
        x, zh, y = place()
        right, left = device(x, zh, (y + 1) % Y), device(x, zh, (y + Y - 1) % Y)
        self.steps = []
        for s in range(Y // 2):
            first, second = blocks.at[(y + Y - s) % Y], blocks.at[(y + s) % Y]
            if s == Y // 2 - 1:
                first, second = first.at[:, :cut], second.at[:, cut:]
            self.steps.append(
                (
                    remote(first, first, right_send.at[s], right_recv.at[s], right),
                    remote(second, second, left_send.at[s], left_recv.at[s], left),
                )
            )

    def start(self, s):
        for copy in self.steps[s]:
            copy.start()

    def wait(self, s):
        for copy in self.steps[s]:
            copy.wait()


class Sum:
    def __init__(self, g_ref, out_ref, own, pre, land, part, ld, ps, pr, is_, ir, os_, or_, cs, cr):
        w = lax.axis_index("wide")
        zl, core = w // 2, w % 2
        half = g_ref.shape[1] // 2
        size = half // CHUNKS
        low = zl < ZL // 2
        edge = (zl == 0) | (zl == ZL - 1)
        mid = (zl == ZL // 2 - 1) | (zl == ZL // 2)
        inward = at_wide(jnp.where(low, w + 2, w - 2))
        outward = at_wide(jnp.where(edge, w, jnp.where(low, w - 2, w + 2)))
        other = at_wide(w + 1 - 2 * core)
        self.edge, self.mid, self.inner = edge, mid, jnp.logical_not(edge | mid)
        self.core, self.inward, self.outward, self.other = core, inward, outward, other
        self.out_ref, self.own, self.pre, self.land, self.part = out_ref, own, pre, land, part

        def span(core_of, k):
            return pl.ds(pl.multiple_of(core_of * half + k * size, size), size)

        def load(k):
            return pltpu.make_async_copy(g_ref.at[:, span(core, k)], own.at[k], ld.at[k])

        def pre_copy(k):
            return remote(g_ref.at[:, span(1 - core, k)], pre.at[k], ps.at[k], pr.at[k], other)

        def in_copy(k, slot):
            return remote(part.at[k], land.at[slot, k], is_.at[k], ir.at[slot, k], inward)

        def out_copy(k):
            cut = out_ref.at[core, k]
            return remote(cut, cut, os_.at[k], or_.at[k], outward)

        def core_copy(k, which):
            cut = out_ref.at[which, k]
            return remote(cut, cut, cs.at[k], cr.at[k], other)

        self.load, self.pre_copy, self.in_copy, self.out_copy, self.core_copy = (
            load, pre_copy, in_copy, out_copy, core_copy,
        )

    def greet(self):
        signal(self.inward)
        signal(self.other)
        pl.when(jnp.logical_not(self.edge))(lambda: signal(self.outward))
        return jnp.where(self.edge, 2, 3)

    def start(self):
        for k in range(CHUNKS):
            self.pre_copy(k).start()

    def edge_in(self):
        @pl.when(self.edge)
        def _():
            for k in range(CHUNKS):
                self.load(k).wait()
                self.pre_copy(k).wait_recv()
                self.part[k] = (self.own[k].astype(f32) + self.pre[k].astype(f32)).astype(bf16)
                self.in_copy(k, 0).start()

    def pass_in(self, role, slot, k):
        @pl.when(role)
        def _():
            self.load(k).wait()
            self.pre_copy(k).wait_recv()
            total = self.own[k].astype(f32) + self.pre[k].astype(f32)
            self.in_copy(k, 0).wait_recv()
            self.part[k] = (total + self.land[0, k].astype(f32)).astype(bf16)
            self.in_copy(k, slot).start()

    def inner_in(self, k):
        self.pass_in(self.inner, 0, k)

    def mid_in(self, k):
        self.pass_in(self.mid, 1, k)

    def middle(self, k):
        @pl.when(self.mid)
        def _():
            self.in_copy(k, 1).wait_recv()
            total = self.part[k].astype(f32) + self.land[1, k].astype(f32)
            self.out_ref[pl.ds(self.core, 1), k] = total.astype(bf16)[None]
            self.out_copy(k).start()
            self.core_copy(k, self.core).start()

    def inner_out(self, k):
        @pl.when(self.inner)
        def _():
            self.out_copy(k).wait_recv()
            self.out_copy(k).start()
            self.core_copy(k, self.core).start()

    def edge_out(self, k):
        @pl.when(self.edge)
        def _():
            self.out_copy(k).wait_recv()
            self.core_copy(k, self.core).start()

    def finish(self):
        for k in range(CHUNKS):
            self.pre_copy(k).wait_send()
            self.in_copy(k, 0).wait_send()
            self.core_copy(k, self.core).wait_send()

        @pl.when(jnp.logical_not(self.edge))
        def _():
            for k in range(CHUNKS):
                self.out_copy(k).wait_send()


def adam(grad, master, moment_one, moment_two):
    one = beta_first * moment_one + (1.0 - beta_first) * grad
    two = beta_second * moment_two + (1.0 - beta_second) * grad * grad
    step_dir = one * (1.0 / bias_first) / (jnp.sqrt(two * (1.0 / bias_second)) + adam_eps)
    return one, two, master - learn_rate * step_dir


def main_kernel(
    tok_any, ids_any, gate_any, g_ref, p_ref, one_ref, two_ref, w_ref,
    newp_ref, newone_ref, newtwo_ref, out_ref,
    tok_ref, ids_ref, gate_ref, own, landing, wide_rows, gathered, w_raw, w_tmp, w_both,
    sum_ref, final, q_first, q_last, rows_first, rows_last,
    hid_own, hid_all, acc, sent, came, turned,
    ld, sems, rs, rr, ls, lr, hsems, ys, yr, cs, cr, s1, r1, s2, r2, *rest
):
    x, zh, y = place()
    w = lax.axis_index("wide")
    core = w % 2
    other = at_wide(w + 1 - 2 * core)
    expert = x * ZH + zh
    rows, columns = p_ref.shape
    half = columns // 2
    width = tok_any.shape[1]
    per = EXPERTS // 2
    batches, fit = 2, per // 2
    q_send, rows_all = (q_first, q_last), (rows_first, rows_last)
    adding = Sum(g_ref, sum_ref, *rest)

    count = adding.greet()
    column = [device(x, zh, (y + k) % Y) for k in range(1, Y)]
    plane = []
    for k in range(1, XZ):
        to = (expert + k) % XZ
        plane.append(device(to // ZH, to % ZH, y))
    for where in column + plane:
        signal(where)

    small_loads = [
        pltpu.make_async_copy(tok_any, tok_ref, ld.at[7]),
        pltpu.make_async_copy(ids_any, ids_ref, ld.at[8]),
        pltpu.make_async_copy(gate_any, gate_ref, ld.at[9]),
    ]
    for copy in small_loads:
        copy.start()
    w_load = pltpu.make_async_copy(w_ref, w_raw, ld.at[0])
    state_loads = []
    for i, which in enumerate((core, 1 - core)):
        span = pl.ds(pl.multiple_of(which * half, half), half)
        for n, (src, dst) in enumerate(
            ((p_ref, newp_ref), (one_ref, newone_ref), (two_ref, newtwo_ref))
        ):
            state_loads.append(
                pltpu.make_async_copy(src.at[:, span], dst.at[:, span], ld.at[1 + i * 3 + n])
            )
    for k in range(CHUNKS):
        adding.load(k).start()
    w_load.start()
    for copy in state_loads:
        copy.start()

    for copy in small_loads:
        copy.wait()
    own[:, :width] = tok_ref[...]
    lane = lax.broadcasted_iota(jnp.int32, (2, QBLOCK), 1)
    weights = jnp.zeros((2, QBLOCK), f32)
    for k in range(ids_ref.shape[1]):
        gate = gate_ref[:, k : k + 1].astype(f32)
        weights += jnp.where(ids_ref[:, k : k + 1] == lane, gate, 0.0)
    own[:, width:] = weights.astype(bf16)
    pl.semaphore_wait(pltpu.get_barrier_semaphore(), count + len(column) + len(plane))

    gather = Gather(own, landing, sems)
    ring = Ring(gathered, own.shape[1] // 256 * 128, rs, rr, ls, lr)
    gather.start()
    adding.start()
    adding.edge_in()

    w_load.wait()
    piece = w_tmp.shape[0]

    def split(i, carry):
        w_tmp[...] = w_raw[pl.ds(pl.multiple_of(i * piece, piece), piece), :].astype(f32)
        to = pl.ds(pl.multiple_of(i * (piece // 2), piece // 2), piece // 2)
        w_both[to, :QBLOCK] = w_tmp[pl.ds(0, piece // 2, stride=2), :].astype(bf16)
        w_both[to, QBLOCK:] = w_tmp[pl.ds(1, piece // 2, stride=2), :].astype(bf16)
        return carry

    lax.fori_loop(0, w_raw.shape[0] // piece, split, 0)

    gather.turn()
    adding.inner_in(0)
    gather.finish()
    for j in range(XZ):
        for i in range(2):
            wide_rows[i * XZ + j : i * XZ + j + 1, :] = landing[j, i : i + 1, :].astype(f32)
    gathered[pl.ds(y, 1)] = wide_rows[...].astype(bf16)[None]
    ring.start(0)
    for copy in state_loads:
        copy.wait()

    def advance(which, k, b):
        at = which * half + (k * Y + b) * QBLOCK
        cut = pl.ds(pl.multiple_of(at, QBLOCK), QBLOCK)
        one, two, updated = adam(
            sum_ref[which, k, :, b * QBLOCK : (b + 1) * QBLOCK].astype(f32),
            newp_ref[:, cut].astype(f32),
            newone_ref[:, cut],
            newtwo_ref[:, cut],
        )
        newone_ref[:, cut] = one
        newtwo_ref[:, cut] = two
        newp_ref[:, cut] = updated.astype(bf16)
        return updated

    def quantize(k):
        for b in range(Y):
            updated = advance(core, k, b)
            amax = jnp.max(jnp.abs(updated), axis=1, keepdims=True)
            scale = ((amax + amax_eps) / quant_limit).astype(bf16)
            quanta = (updated * (1.0 / scale.astype(f32))).astype(bf16)
            spot = k % fit
            q_send[k // fit][b, :, spot * QBLOCK : (spot + 1) * QBLOCK] = quanta
            q_send[1][b, :, fit * QBLOCK + k : fit * QBLOCK + k + 1] = scale

    order = [1, 7, 2, 6, 3, 5, 4]

    def relay(batch, k):
        return remote(
            q_send[batch].at[(y + k) % Y], rows_all[batch].at[core, y],
            ys.at[batch, k], yr.at[batch, k], column[k - 1],
        )

    def mine(batch):
        return pltpu.make_async_copy(
            q_send[batch].at[y], rows_all[batch].at[core, y], ys.at[batch, 0]
        )

    def relay_start(batch):
        for k in order:
            relay(batch, k).start()
        mine(batch).start()

    def share(batch, which):
        part = rows_all[batch].at[which]
        return remote(part, part, cs.at[batch], cr.at[batch], other)

    def relay_finish(batch):
        mine(batch).wait()
        for k in order:
            relay(batch, k).wait_recv()
        share(batch, core).start()

    adding.inner_in(1)
    adding.inner_in(2)
    adding.mid_in(0)
    adding.mid_in(1)
    ring.wait(0)
    ring.start(1)
    adding.inner_in(3)
    adding.mid_in(2)
    adding.middle(0)
    adding.middle(1)
    adding.mid_in(3)
    ring.wait(1)
    ring.start(2)
    adding.middle(2)
    adding.middle(3)
    adding.inner_out(0)
    adding.inner_out(1)
    ring.wait(2)
    ring.start(3)
    adding.inner_out(2)
    adding.inner_out(3)
    adding.edge_out(0)
    quantize(0)
    adding.edge_out(1)
    quantize(1)
    relay_start(0)
    ring.wait(3)

    tokens = gathered.reshape(Y * 16, own.shape[1])
    proj = jnp.dot(tokens[:, :width], w_both[...], preferred_element_type=f32)
    weight = tokens[:, width:].astype(f32)
    lanes = lax.broadcasted_iota(jnp.int32, weight.shape, 1)
    weight = jnp.sum(jnp.where(lanes == expert, weight, 0.0), axis=1, keepdims=True)
    gate = proj[:, :QBLOCK]
    hidden = weight * (gate * jax.nn.sigmoid(gate)) * proj[:, QBLOCK:]
    hid_own[...] = jnp.transpose(hidden).astype(bf16)
    hid_gather = Gather(hid_own, hid_all, hsems)
    hid_gather.start()
    adding.edge_out(2)
    quantize(2)
    adding.edge_out(3)
    quantize(3)
    relay_start(1)
    relay_finish(0)
    hid_gather.turn()
    relay_finish(1)
    hid_gather.finish()

    def products(which, j):
        total = None
        for e in range(per):
            spot = e % fit
            quanta = rows_all[e // fit][which, j, :, spot * QBLOCK : (spot + 1) * QBLOCK]
            scale = rows_all[1][which, j, :, fit * QBLOCK + e : fit * QBLOCK + e + 1].astype(f32)
            term = scale * jnp.dot(quanta, hid_all[which * per + e], preferred_element_type=f32)
            total = term if total is None else total + term
        return total

    for j in range(Y):
        acc[j, :rows] = products(core, j)
        acc[j, rows:] = jnp.zeros_like(acc[j, rows:])
    for batch in range(batches):
        share(batch, 1 - core).wait_recv()
    for j in range(Y):
        acc[j, :rows] += products(1 - core, j)

    for j in range(Y // 2):
        pair = jnp.concatenate([acc[2 * j], acc[2 * j + 1]], axis=0)
        pair = jnp.transpose(pair).astype(bf16)
        for t in range(Y):
            sent[t, :, j * QBLOCK : (j + 1) * QBLOCK] = pair[t * 16 : (t + 1) * 16]
    copies = []
    for k in order:
        to = (y + k) % Y
        copies.append(remote(sent.at[to], came.at[y], s1.at[k], r1.at[k], column[k - 1]))
        copies[-1].start()
    came[pl.ds(y, 1)] = sent[pl.ds(y, 1)]

    def other_half(k):
        adding.core_copy(k, 1 - core).wait_recv()
        for b in range(Y):
            advance(1 - core, k, b)

    other_half(0)
    other_half(1)
    for copy in copies:
        copy.wait()
    total = came[0].astype(f32)
    for j in range(1, Y):
        total += came[j].astype(f32)
    for i in range(2):
        for q in range(4):
            part = total[i * 8 : (i + 1) * 8, q * 128 : (q + 1) * 128]
            turned[:, i * 4 + q, :] = part
    copies = []
    for k in range(1, XZ):
        to = (expert + k) % XZ
        copies.append(remote(turned.at[to], final.at[expert], s2.at[k], r2.at[k], plane[k - 1]))
        copies[-1].start()
    final[pl.ds(expert, 1)] = turned[pl.ds(expert, 1)]
    other_half(2)
    other_half(3)
    for copy in copies:
        copy.wait()
    assemble(final, out_ref, rows)

    for batch in range(batches):
        for k in order:
            relay(batch, k).wait_send()
        share(batch, core).wait_send()
    adding.finish()


def assemble(final, out_ref, rows):
    lane = lax.broadcasted_iota(jnp.int32, (2, 128), 1)
    pieces = [None] * (out_ref.shape[1] // 128)

    def add(tile, value):
        pieces[tile] = value if pieces[tile] is None else pieces[tile] + value

    for j in range(XZ):
        for q in range(4):
            pair = final[j, pl.ds(q, 2, stride=4), :]
            closed = jnp.where(lane < rows, pair, pltpu.roll(pair, 64 + rows, 1))
            closed = jnp.where(lane < 2 * rows, closed, 0.0)
            tile, shift = divmod((j * 4 + q) * 2 * rows, 128)
            turned = pltpu.roll(closed, shift, 1) if shift else closed
            add(tile, jnp.where(lane >= shift, turned, 0.0))
            if shift + 2 * rows > 128:
                add(tile + 1, jnp.where(lane < shift, turned, 0.0))
    for tile, value in enumerate(pieces):
        out_ref[:, tile * 128 : (tile + 1) * 128] = value.astype(bf16)


def store_kernel(*refs):
    sources, targets, sems = refs[:4], refs[4:8], refs[8]
    copies = [
        pltpu.make_async_copy(src, dst, sems.at[i]) for i, (src, dst) in enumerate(zip(sources, targets))
    ]
    for copy in copies:
        copy.start()
    for copy in copies:
        copy.wait()


def body(grad_parts, master, moment_one, moment_two, gate_up, tokens, expert_ids, gate_vals):
    shape = jax.ShapeDtypeStruct
    rows, columns = master.shape
    width = tokens.shape[1]
    full = width + QBLOCK
    size = columns // 2 // CHUNKS
    tok = Y * 16
    sem = DMA((CHUNKS,))
    chunk = pltpu.VMEM((CHUNKS, rows, size), bf16)
    results = pl.pallas_call(
        main_kernel,
        out_shape=(
            shape((rows, columns), bf16),
            shape((rows, columns), f32),
            shape((rows, columns), f32),
            shape((2, width), bf16),
        ),
        in_specs=[HBM] * 8,
        out_specs=(VMEM,) * 4,
        scratch_shapes=[
            pltpu.VMEM(tokens.shape, bf16),
            pltpu.VMEM(expert_ids.shape, jnp.int32),
            pltpu.VMEM(gate_vals.shape, bf16),
            pltpu.VMEM((2, full), bf16),
            pltpu.VMEM((XZ, 2, full), bf16),
            pltpu.VMEM((16, full), f32),
            pltpu.VMEM((Y, 16, full), bf16),
            pltpu.VMEM((2 * width, QBLOCK), bf16),
            pltpu.VMEM((512, QBLOCK), f32),
            pltpu.VMEM((width, 2 * QBLOCK), bf16),
            pltpu.VMEM((2, CHUNKS, rows, size), bf16),
            pltpu.VMEM((XZ, 8, 128), f32),
            pltpu.VMEM((Y, rows, 2 * QBLOCK), bf16),
            pltpu.VMEM((Y, rows, 3 * QBLOCK), bf16),
            pltpu.VMEM((2, Y, rows, 2 * QBLOCK), bf16),
            pltpu.VMEM((2, Y, rows, 3 * QBLOCK), bf16),
            pltpu.VMEM((QBLOCK, tok), bf16),
            pltpu.VMEM((XZ, QBLOCK, tok), bf16),
            pltpu.VMEM((Y, 64, tok), f32),
            pltpu.VMEM((Y, 16, 512), bf16),
            pltpu.VMEM((Y, 16, 512), bf16),
            pltpu.VMEM((XZ, 8, 128), f32),
            DMA((10,)),
        ]
        + GATHER_SEMS
        + RING_SEMS
        + GATHER_SEMS
        + [DMA((2, 8)), DMA((2, 8)), DMA((2,)), DMA((2,)), DMA((8,)), DMA((8,)), DMA((8,)), DMA((8,))]
        + [chunk, chunk, pltpu.VMEM((2, CHUNKS, rows, size), bf16), chunk]
        + [sem, sem, sem, sem, DMA((2, CHUNKS)), sem, sem, sem, sem],
        compiler_params=pltpu.CompilerParams(
            collective_id=0, has_side_effects=True, vmem_limit_bytes=36 * 2**20
        ),
    )(
        *[
            pltpu.with_memory_space_constraint(value, pltpu.HBM)
            for value in (
                tokens, expert_ids, gate_vals, grad_parts[0], master, moment_one, moment_two,
                gate_up.reshape(2 * width, QBLOCK),
            )
        ]
    )

    anywhere = pl.BlockSpec(memory_space=pl.ANY)
    return pl.pallas_call(
        store_kernel,
        out_shape=tuple(shape(value.shape, value.dtype) for value in results),
        in_specs=[VMEM] * 4,
        out_specs=(anywhere,) * 4,
        scratch_shapes=[DMA((4,))],
        compiler_params=pltpu.CompilerParams(vmem_limit_bytes=16 * 2**20),
    )(*results)


def solution(mesh):
    in_specs = (
        P("wide", "narrow", None),
        P("narrow", None),
        P("narrow", None),
        P("narrow", None),
        P(None, None, "narrow"),
        P(("wide", "narrow"), None),
        P(("wide", "narrow"), None),
        P(("wide", "narrow"), None),
    )
    out_specs = (
        P("narrow", None),
        P("narrow", None),
        P("narrow", None),
        P(("wide", "narrow"), None),
    )
    return jax.shard_map(body, mesh=mesh, in_specs=in_specs, out_specs=out_specs, check_vma=False)
```

```python
import jax
import jax.numpy as jnp
from jax import lax
from jax.experimental import pallas as pl
from jax.experimental.pallas import tpu as pltpu
from jax.sharding import PartitionSpec as P

EXPERTS = 8
QBLOCK = 128
X, ZH, Y = 4, 2, 8
XZ = X * ZH
ZL = 6
CHUNKS = 4

beta_first = 0.9
beta_second = 0.95
learn_rate = 0.003
adam_eps = 1e-08
quant_limit = 448.0
amax_eps = 1e-06
bias_first = 1.0 - 0.9**10
bias_second = 1.0 - 0.95**10

VMEM = pl.BlockSpec(memory_space=pltpu.VMEM)
HBM = pl.BlockSpec(memory_space=pltpu.HBM)
DMA = pltpu.SemaphoreType.DMA
f32 = jnp.float32
bf16 = jnp.bfloat16


def at_wide(index):
    return {"wide": index}


def remote(src, dst, send, recv, where):
    return pltpu.make_async_remote_copy(
        src_ref=src,
        dst_ref=dst,
        send_sem=send,
        recv_sem=recv,
        device_id=where,
        device_id_type=pl.DeviceIdType.MESH,
    )


def signal(where):
    pl.semaphore_signal(
        pltpu.get_barrier_semaphore(), inc=1, device_id=where, device_id_type=pl.DeviceIdType.MESH
    )


def place():
    n = lax.axis_index("narrow")
    return n // (ZH * Y), (n // Y) % ZH, n % Y


def device(x, zh, y):
    w = lax.axis_index("wide")
    own = (lax.axis_index("narrow") // Y) % ZH
    mirrored = (ZL - 1 - w // 2) * 2 + w % 2
    return {"wide": jnp.where(zh == own, w, mirrored), "narrow": (x * ZH + zh) * Y + y}


GATHER_SEMS = [DMA((9,))]
RING_SEMS = [DMA((4,)), DMA((4,)), DMA((4,)), DMA((4,))]


class Gather:
    def __init__(self, own, landing, sems):
        x, zh, y = place()
        me = x * ZH + zh
        self.local = pltpu.make_async_copy(own, landing.at[me], sems.at[8])
        self.cross = remote(own, landing.at[me], sems.at[0], sems.at[1], device(x, 1 - zh, y))
        pair = landing.at[pl.ds(x * ZH, ZH)]
        self.along = [
            remote(pair, pair, sems.at[1 + k], sems.at[4 + k], device((x + k) % X, zh, y))
            for k in (2, 1, 3)
        ]

    def start(self):
        self.cross.start()
        self.local.start()

    def turn(self):
        self.local.wait()
        self.cross.wait()
        for copy in self.along:
            copy.start()

    def finish(self):
        for copy in self.along:
            copy.wait()


class Ring:
    def __init__(self, blocks, cut, right_send, right_recv, left_send, left_recv):
        x, zh, y = place()
        right, left = device(x, zh, (y + 1) % Y), device(x, zh, (y + Y - 1) % Y)
        self.steps = []
        for s in range(Y // 2):
            first, second = blocks.at[(y + Y - s) % Y], blocks.at[(y + s) % Y]
            if s == Y // 2 - 1:
                first, second = first.at[:, :cut], second.at[:, cut:]
            self.steps.append(
                (
                    remote(first, first, right_send.at[s], right_recv.at[s], right),
                    remote(second, second, left_send.at[s], left_recv.at[s], left),
                )
            )

    def start(self, s):
        for copy in self.steps[s]:
            copy.start()

    def wait(self, s):
        for copy in self.steps[s]:
            copy.wait()


class Sum:
    def __init__(self, g_ref, out_ref, own, pre, land, part, ld, ps, pr, is_, ir, os_, or_, cs, cr):
        w = lax.axis_index("wide")
        zl, core = w // 2, w % 2
        half = g_ref.shape[1] // 2
        size = half // CHUNKS
        low = zl < ZL // 2
        edge = (zl == 0) | (zl == ZL - 1)
        mid = (zl == ZL // 2 - 1) | (zl == ZL // 2)
        inward = at_wide(jnp.where(low, w + 2, w - 2))
        outward = at_wide(jnp.where(edge, w, jnp.where(low, w - 2, w + 2)))
        other = at_wide(w + 1 - 2 * core)
        self.edge, self.mid, self.inner = edge, mid, jnp.logical_not(edge | mid)
        self.core, self.inward, self.outward, self.other = core, inward, outward, other
        self.out_ref, self.own, self.pre, self.land, self.part = out_ref, own, pre, land, part

        def span(core_of, k):
            return pl.ds(pl.multiple_of(core_of * half + k * size, size), size)

        def load(k):
            return pltpu.make_async_copy(g_ref.at[:, span(core, k)], own.at[k], ld.at[k])

        def pre_copy(k):
            return remote(g_ref.at[:, span(1 - core, k)], pre.at[k], ps.at[k], pr.at[k], other)

        def in_copy(k, slot):
            return remote(part.at[k], land.at[slot, k], is_.at[k], ir.at[slot, k], inward)

        def out_copy(k):
            cut = out_ref.at[core, k]
            return remote(cut, cut, os_.at[k], or_.at[k], outward)

        def core_copy(k, which):
            cut = out_ref.at[which, k]
            return remote(cut, cut, cs.at[k], cr.at[k], other)

        self.load, self.pre_copy, self.in_copy, self.out_copy, self.core_copy = (
            load, pre_copy, in_copy, out_copy, core_copy,
        )

    def greet(self):
        signal(self.inward)
        signal(self.other)
        pl.when(jnp.logical_not(self.edge))(lambda: signal(self.outward))
        return jnp.where(self.edge, 2, 3)

    def start(self):
        for k in range(CHUNKS):
            self.pre_copy(k).start()

    def edge_in(self):
        @pl.when(self.edge)
        def _():
            for k in range(CHUNKS):
                self.load(k).wait()
                self.pre_copy(k).wait_recv()
                self.part[k] = (self.own[k].astype(f32) + self.pre[k].astype(f32)).astype(bf16)
                self.in_copy(k, 0).start()

    def pass_in(self, role, slot, k):
        @pl.when(role)
        def _():
            self.load(k).wait()
            self.pre_copy(k).wait_recv()
            total = self.own[k].astype(f32) + self.pre[k].astype(f32)
            self.in_copy(k, 0).wait_recv()
            self.part[k] = (total + self.land[0, k].astype(f32)).astype(bf16)
            self.in_copy(k, slot).start()

    def inner_in(self, k):
        self.pass_in(self.inner, 0, k)

    def mid_in(self, k):
        self.pass_in(self.mid, 1, k)

    def middle(self, k):
        @pl.when(self.mid)
        def _():
            self.in_copy(k, 1).wait_recv()
            total = self.part[k].astype(f32) + self.land[1, k].astype(f32)
            self.out_ref[pl.ds(self.core, 1), k] = total.astype(bf16)[None]
            self.out_copy(k).start()
            self.core_copy(k, self.core).start()

    def inner_out(self, k):
        @pl.when(self.inner)
        def _():
            self.out_copy(k).wait_recv()
            self.out_copy(k).start()
            self.core_copy(k, self.core).start()

    def edge_out(self, k):
        @pl.when(self.edge)
        def _():
            self.out_copy(k).wait_recv()
            self.core_copy(k, self.core).start()

    def finish(self):
        for k in range(CHUNKS):
            self.pre_copy(k).wait_send()
            self.in_copy(k, 0).wait_send()
            self.core_copy(k, self.core).wait_send()

        @pl.when(jnp.logical_not(self.edge))
        def _():
            for k in range(CHUNKS):
                self.out_copy(k).wait_send()


def adam(grad, master, moment_one, moment_two):
    one = beta_first * moment_one + (1.0 - beta_first) * grad
    two = beta_second * moment_two + (1.0 - beta_second) * grad * grad
    step_dir = one * (1.0 / bias_first) / (jnp.sqrt(two * (1.0 / bias_second)) + adam_eps)
    return one, two, master - learn_rate * step_dir


def main_kernel(
    tok_any, ids_any, gate_any, g_ref, p_ref, one_ref, two_ref, w_ref,
    newp_ref, newone_ref, newtwo_ref, out_ref,
    tok_ref, ids_ref, gate_ref, own, landing, wide_rows, gathered, w_raw, w_tmp, w_both,
    sum_ref, final, q_first, q_last, rows_first, rows_last,
    hid_own, hid_all, acc, sent, came, turned,
    ld, sems, rs, rr, ls, lr, hsems, ys, yr, cs, cr, s1, r1, s2, r2, *rest
):
    x, zh, y = place()
    w = lax.axis_index("wide")
    core = w % 2
    other = at_wide(w + 1 - 2 * core)
    expert = x * ZH + zh
    rows, columns = p_ref.shape
    half = columns // 2
    width = tok_any.shape[1]
    per = EXPERTS // 2
    batches, fit = 2, per // 2
    q_send, rows_all = (q_first, q_last), (rows_first, rows_last)
    adding = Sum(g_ref, sum_ref, *rest)

    count = adding.greet()
    column = [device(x, zh, (y + k) % Y) for k in range(1, Y)]
    plane = []
    for k in range(1, XZ):
        to = (expert + k) % XZ
        plane.append(device(to // ZH, to % ZH, y))
    for where in column + plane:
        signal(where)

    small_loads = [
        pltpu.make_async_copy(tok_any, tok_ref, ld.at[7]),
        pltpu.make_async_copy(ids_any, ids_ref, ld.at[8]),
        pltpu.make_async_copy(gate_any, gate_ref, ld.at[9]),
    ]
    for copy in small_loads:
        copy.start()
    w_load = pltpu.make_async_copy(w_ref, w_raw, ld.at[0])
    state_loads = []
    for i, which in enumerate((core, 1 - core)):
        span = pl.ds(pl.multiple_of(which * half, half), half)
        for n, (src, dst) in enumerate(
            ((p_ref, newp_ref), (one_ref, newone_ref), (two_ref, newtwo_ref))
        ):
            state_loads.append(
                pltpu.make_async_copy(src.at[:, span], dst.at[:, span], ld.at[1 + i * 3 + n])
            )
    for k in range(CHUNKS):
        adding.load(k).start()
    w_load.start()
    for copy in state_loads:
        copy.start()

    for copy in small_loads:
        copy.wait()
    own[:, :width] = tok_ref[...]
    lane = lax.broadcasted_iota(jnp.int32, (2, QBLOCK), 1)
    weights = jnp.zeros((2, QBLOCK), f32)
    for k in range(ids_ref.shape[1]):
        gate = gate_ref[:, k : k + 1].astype(f32)
        weights += jnp.where(ids_ref[:, k : k + 1] == lane, gate, 0.0)
    own[:, width:] = weights.astype(bf16)
    pl.semaphore_wait(pltpu.get_barrier_semaphore(), count + len(column) + len(plane))

    gather = Gather(own, landing, sems)
    ring = Ring(gathered, own.shape[1] // 256 * 128, rs, rr, ls, lr)
    gather.start()
    adding.start()
    adding.edge_in()

    w_load.wait()
    piece = w_tmp.shape[0]

    def split(i, carry):
        w_tmp[...] = w_raw[pl.ds(pl.multiple_of(i * piece, piece), piece), :].astype(f32)
        to = pl.ds(pl.multiple_of(i * (piece // 2), piece // 2), piece // 2)
        w_both[to, :QBLOCK] = w_tmp[pl.ds(0, piece // 2, stride=2), :].astype(bf16)
        w_both[to, QBLOCK:] = w_tmp[pl.ds(1, piece // 2, stride=2), :].astype(bf16)
        return carry

    lax.fori_loop(0, w_raw.shape[0] // piece, split, 0)

    gather.turn()
    adding.inner_in(0)
    gather.finish()
    for j in range(XZ):
        for i in range(2):
            wide_rows[i * XZ + j : i * XZ + j + 1, :] = landing[j, i : i + 1, :].astype(f32)
    gathered[pl.ds(y, 1)] = wide_rows[...].astype(bf16)[None]
    ring.start(0)
    for copy in state_loads:
        copy.wait()

    def advance(which, k, b):
        at = which * half + (k * Y + b) * QBLOCK
        cut = pl.ds(pl.multiple_of(at, QBLOCK), QBLOCK)
        one, two, updated = adam(
            sum_ref[which, k, :, b * QBLOCK : (b + 1) * QBLOCK].astype(f32),
            newp_ref[:, cut].astype(f32),
            newone_ref[:, cut],
            newtwo_ref[:, cut],
        )
        newone_ref[:, cut] = one
        newtwo_ref[:, cut] = two
        newp_ref[:, cut] = updated.astype(bf16)
        return updated

    def quantize(k):
        for b in range(Y):
            updated = advance(core, k, b)
            amax = jnp.max(jnp.abs(updated), axis=1, keepdims=True)
            scale = ((amax + amax_eps) / quant_limit).astype(bf16)
            quanta = (updated * (1.0 / scale.astype(f32))).astype(bf16)
            spot = k % fit
            q_send[k // fit][b, :, spot * QBLOCK : (spot + 1) * QBLOCK] = quanta
            q_send[1][b, :, fit * QBLOCK + k : fit * QBLOCK + k + 1] = scale

    order = [4, 3, 5, 2, 6, 1, 7]

    def relay(batch, k):
        return remote(
            q_send[batch].at[(y + k) % Y], rows_all[batch].at[core, y],
            ys.at[batch, k], yr.at[batch, k], column[k - 1],
        )

    def mine(batch):
        return pltpu.make_async_copy(
            q_send[batch].at[y], rows_all[batch].at[core, y], ys.at[batch, 0]
        )

    def relay_start(batch):
        for k in order:
            relay(batch, k).start()
        mine(batch).start()

    def share(batch, which):
        part = rows_all[batch].at[which]
        return remote(part, part, cs.at[batch], cr.at[batch], other)

    def relay_finish(batch):
        mine(batch).wait()
        for k in order:
            relay(batch, k).wait_recv()
        share(batch, core).start()

    adding.inner_in(1)
    adding.inner_in(2)
    adding.mid_in(0)
    adding.mid_in(1)
    ring.wait(0)
    ring.start(1)
    adding.inner_in(3)
    adding.mid_in(2)
    adding.middle(0)
    adding.middle(1)
    adding.mid_in(3)
    ring.wait(1)
    ring.start(2)
    adding.middle(2)
    adding.middle(3)
    adding.inner_out(0)
    adding.inner_out(1)
    ring.wait(2)
    ring.start(3)
    adding.inner_out(2)
    adding.inner_out(3)
    adding.edge_out(0)
    quantize(0)
    adding.edge_out(1)
    quantize(1)
    relay_start(0)
    ring.wait(3)

    tokens = gathered.reshape(Y * 16, own.shape[1])
    proj = jnp.dot(tokens[:, :width], w_both[...], preferred_element_type=f32)
    weight = tokens[:, width:].astype(f32)
    lanes = lax.broadcasted_iota(jnp.int32, weight.shape, 1)
    weight = jnp.sum(jnp.where(lanes == expert, weight, 0.0), axis=1, keepdims=True)
    gate = proj[:, :QBLOCK]
    hidden = weight * (gate * jax.nn.sigmoid(gate)) * proj[:, QBLOCK:]
    hid_own[...] = jnp.transpose(hidden).astype(bf16)
    hid_gather = Gather(hid_own, hid_all, hsems)
    hid_gather.start()
    adding.edge_out(2)
    quantize(2)
    adding.edge_out(3)
    quantize(3)
    relay_start(1)
    relay_finish(0)
    hid_gather.turn()
    relay_finish(1)
    hid_gather.finish()

    def products(which, j):
        total = None
        for e in range(per):
            spot = e % fit
            quanta = rows_all[e // fit][which, j, :, spot * QBLOCK : (spot + 1) * QBLOCK]
            scale = rows_all[1][which, j, :, fit * QBLOCK + e : fit * QBLOCK + e + 1].astype(f32)
            term = scale * jnp.dot(quanta, hid_all[which * per + e], preferred_element_type=f32)
            total = term if total is None else total + term
        return total

    for j in range(Y):
        acc[j, :rows] = products(core, j)
        acc[j, rows:] = jnp.zeros_like(acc[j, rows:])
    for batch in range(batches):
        share(batch, 1 - core).wait_recv()
    for j in range(Y):
        acc[j, :rows] += products(1 - core, j)

    for j in range(Y // 2):
        pair = jnp.concatenate([acc[2 * j], acc[2 * j + 1]], axis=0)
        pair = jnp.transpose(pair).astype(bf16)
        for t in range(Y):
            sent[t, :, j * QBLOCK : (j + 1) * QBLOCK] = pair[t * 16 : (t + 1) * 16]
    copies = []
    for k in order:
        to = (y + k) % Y
        copies.append(remote(sent.at[to], came.at[y], s1.at[k], r1.at[k], column[k - 1]))
        copies[-1].start()
    came[pl.ds(y, 1)] = sent[pl.ds(y, 1)]

    def other_half(k):
        adding.core_copy(k, 1 - core).wait_recv()
        for b in range(Y):
            advance(1 - core, k, b)

    other_half(0)
    other_half(1)
    for copy in copies:
        copy.wait()
    total = came[0].astype(f32)
    for j in range(1, Y):
        total += came[j].astype(f32)
    for i in range(2):
        for q in range(4):
            part = total[i * 8 : (i + 1) * 8, q * 128 : (q + 1) * 128]
            turned[:, i * 4 + q, :] = part
    copies = []
    for k in (3, 5, 1, 7, 4, 2, 6):
        to = (expert + k) % XZ
        copies.append(remote(turned.at[to], final.at[expert], s2.at[k], r2.at[k], plane[k - 1]))
        copies[-1].start()
    final[pl.ds(expert, 1)] = turned[pl.ds(expert, 1)]
    other_half(2)
    other_half(3)
    for copy in copies:
        copy.wait()
    assemble(final, out_ref, rows)

    for batch in range(batches):
        for k in order:
            relay(batch, k).wait_send()
        share(batch, core).wait_send()
    adding.finish()


def assemble(final, out_ref, rows):
    lane = lax.broadcasted_iota(jnp.int32, (2, 128), 1)
    pieces = [None] * (out_ref.shape[1] // 128)

    def add(tile, value):
        pieces[tile] = value if pieces[tile] is None else pieces[tile] + value

    for j in range(XZ):
        for q in range(4):
            pair = final[j, pl.ds(q, 2, stride=4), :]
            closed = jnp.where(lane < rows, pair, pltpu.roll(pair, 64 + rows, 1))
            closed = jnp.where(lane < 2 * rows, closed, 0.0)
            tile, shift = divmod((j * 4 + q) * 2 * rows, 128)
            turned = pltpu.roll(closed, shift, 1) if shift else closed
            add(tile, jnp.where(lane >= shift, turned, 0.0))
            if shift + 2 * rows > 128:
                add(tile + 1, jnp.where(lane < shift, turned, 0.0))
    for tile, value in enumerate(pieces):
        out_ref[:, tile * 128 : (tile + 1) * 128] = value.astype(bf16)


def store_kernel(*refs):
    sources, targets, sems = refs[:4], refs[4:8], refs[8]
    copies = [
        pltpu.make_async_copy(src, dst, sems.at[i]) for i, (src, dst) in enumerate(zip(sources, targets))
    ]
    for copy in copies:
        copy.start()
    for copy in copies:
        copy.wait()


def body(grad_parts, master, moment_one, moment_two, gate_up, tokens, expert_ids, gate_vals):
    shape = jax.ShapeDtypeStruct
    rows, columns = master.shape
    width = tokens.shape[1]
    full = width + QBLOCK
    size = columns // 2 // CHUNKS
    tok = Y * 16
    sem = DMA((CHUNKS,))
    chunk = pltpu.VMEM((CHUNKS, rows, size), bf16)
    results = pl.pallas_call(
        main_kernel,
        out_shape=(
            shape((rows, columns), bf16),
            shape((rows, columns), f32),
            shape((rows, columns), f32),
            shape((2, width), bf16),
        ),
        in_specs=[HBM] * 8,
        out_specs=(VMEM,) * 4,
        scratch_shapes=[
            pltpu.VMEM(tokens.shape, bf16),
            pltpu.VMEM(expert_ids.shape, jnp.int32),
            pltpu.VMEM(gate_vals.shape, bf16),
            pltpu.VMEM((2, full), bf16),
            pltpu.VMEM((XZ, 2, full), bf16),
            pltpu.VMEM((16, full), f32),
            pltpu.VMEM((Y, 16, full), bf16),
            pltpu.VMEM((2 * width, QBLOCK), bf16),
            pltpu.VMEM((512, QBLOCK), f32),
            pltpu.VMEM((width, 2 * QBLOCK), bf16),
            pltpu.VMEM((2, CHUNKS, rows, size), bf16),
            pltpu.VMEM((XZ, 8, 128), f32),
            pltpu.VMEM((Y, rows, 2 * QBLOCK), bf16),
            pltpu.VMEM((Y, rows, 3 * QBLOCK), bf16),
            pltpu.VMEM((2, Y, rows, 2 * QBLOCK), bf16),
            pltpu.VMEM((2, Y, rows, 3 * QBLOCK), bf16),
            pltpu.VMEM((QBLOCK, tok), bf16),
            pltpu.VMEM((XZ, QBLOCK, tok), bf16),
            pltpu.VMEM((Y, 64, tok), f32),
            pltpu.VMEM((Y, 16, 512), bf16),
            pltpu.VMEM((Y, 16, 512), bf16),
            pltpu.VMEM((XZ, 8, 128), f32),
            DMA((10,)),
        ]
        + GATHER_SEMS
        + RING_SEMS
        + GATHER_SEMS
        + [DMA((2, 8)), DMA((2, 8)), DMA((2,)), DMA((2,)), DMA((8,)), DMA((8,)), DMA((8,)), DMA((8,))]
        + [chunk, chunk, pltpu.VMEM((2, CHUNKS, rows, size), bf16), chunk]
        + [sem, sem, sem, sem, DMA((2, CHUNKS)), sem, sem, sem, sem],
        compiler_params=pltpu.CompilerParams(
            collective_id=0, has_side_effects=True, vmem_limit_bytes=36 * 2**20
        ),
    )(
        *[
            pltpu.with_memory_space_constraint(value, pltpu.HBM)
            for value in (
                tokens, expert_ids, gate_vals, grad_parts[0], master, moment_one, moment_two,
                gate_up.reshape(2 * width, QBLOCK),
            )
        ]
    )

    anywhere = pl.BlockSpec(memory_space=pl.ANY)
    return pl.pallas_call(
        store_kernel,
        out_shape=tuple(shape(value.shape, value.dtype) for value in results),
        in_specs=[VMEM] * 4,
        out_specs=(anywhere,) * 4,
        scratch_shapes=[DMA((4,))],
        compiler_params=pltpu.CompilerParams(vmem_limit_bytes=16 * 2**20),
    )(*results)


def solution(mesh):
    in_specs = (
        P("wide", "narrow", None),
        P("narrow", None),
        P("narrow", None),
        P("narrow", None),
        P(None, None, "narrow"),
        P(("wide", "narrow"), None),
        P(("wide", "narrow"), None),
        P(("wide", "narrow"), None),
    )
    out_specs = (
        P("narrow", None),
        P("narrow", None),
        P("narrow", None),
        P(("wide", "narrow"), None),
    )
    return jax.shard_map(body, mesh=mesh, in_specs=in_specs, out_specs=out_specs, check_vma=False)
```

```python
import jax
import jax.numpy as jnp
from jax import lax
from jax.experimental import pallas as pl
from jax.experimental.pallas import tpu as pltpu
from jax.sharding import PartitionSpec as P

EXPERTS = 8
QBLOCK = 128
X, ZH, Y = 4, 2, 8
XZ = X * ZH
ZL = 6
CHUNKS = 4

beta_first = 0.9
beta_second = 0.95
learn_rate = 0.003
adam_eps = 1e-08
quant_limit = 448.0
amax_eps = 1e-06
bias_first = 1.0 - 0.9**10
bias_second = 1.0 - 0.95**10

VMEM = pl.BlockSpec(memory_space=pltpu.VMEM)
HBM = pl.BlockSpec(memory_space=pltpu.HBM)
DMA = pltpu.SemaphoreType.DMA
f32 = jnp.float32
bf16 = jnp.bfloat16


def at_wide(index):
    return {"wide": index}


def remote(src, dst, send, recv, where):
    return pltpu.make_async_remote_copy(
        src_ref=src,
        dst_ref=dst,
        send_sem=send,
        recv_sem=recv,
        device_id=where,
        device_id_type=pl.DeviceIdType.MESH,
    )


def signal(where):
    pl.semaphore_signal(
        pltpu.get_barrier_semaphore(), inc=1, device_id=where, device_id_type=pl.DeviceIdType.MESH
    )


def place():
    n = lax.axis_index("narrow")
    return n // (ZH * Y), (n // Y) % ZH, n % Y


def device(x, zh, y):
    w = lax.axis_index("wide")
    own = (lax.axis_index("narrow") // Y) % ZH
    mirrored = (ZL - 1 - w // 2) * 2 + w % 2
    return {"wide": jnp.where(zh == own, w, mirrored), "narrow": (x * ZH + zh) * Y + y}


GATHER_SEMS = [DMA((9,))]
RING_SEMS = [DMA((4,)), DMA((4,)), DMA((4,)), DMA((4,))]


class Gather:
    def __init__(self, own, landing, sems):
        x, zh, y = place()
        me = x * ZH + zh
        self.local = pltpu.make_async_copy(own, landing.at[me], sems.at[8])
        self.cross = remote(own, landing.at[me], sems.at[0], sems.at[1], device(x, 1 - zh, y))
        pair = landing.at[pl.ds(x * ZH, ZH)]
        self.along = [
            remote(pair, pair, sems.at[1 + k], sems.at[4 + k], device((x + k) % X, zh, y))
            for k in (2, 1, 3)
        ]

    def start(self):
        self.cross.start()
        self.local.start()

    def turn(self):
        self.local.wait()
        self.cross.wait()
        for copy in self.along:
            copy.start()

    def finish(self):
        for copy in self.along:
            copy.wait()


class Ring:
    def __init__(self, blocks, cut, right_send, right_recv, left_send, left_recv):
        x, zh, y = place()
        right, left = device(x, zh, (y + 1) % Y), device(x, zh, (y + Y - 1) % Y)
        self.steps = []
        for s in range(Y // 2):
            first, second = blocks.at[(y + Y - s) % Y], blocks.at[(y + s) % Y]
            if s == Y // 2 - 1:
                first, second = first.at[:, :cut], second.at[:, cut:]
            self.steps.append(
                (
                    remote(first, first, right_send.at[s], right_recv.at[s], right),
                    remote(second, second, left_send.at[s], left_recv.at[s], left),
                )
            )

    def start(self, s):
        for copy in self.steps[s]:
            copy.start()

    def wait(self, s):
        for copy in self.steps[s]:
            copy.wait()


class Sum:
    def __init__(self, g_ref, out_ref, own, pre, land, part, ld, ps, pr, is_, ir, os_, or_, cs, cr):
        w = lax.axis_index("wide")
        zl, core = w // 2, w % 2
        half = g_ref.shape[1] // 2
        size = half // CHUNKS
        low = zl < ZL // 2
        edge = (zl == 0) | (zl == ZL - 1)
        mid = (zl == ZL // 2 - 1) | (zl == ZL // 2)
        inward = at_wide(jnp.where(low, w + 2, w - 2))
        outward = at_wide(jnp.where(edge, w, jnp.where(low, w - 2, w + 2)))
        other = at_wide(w + 1 - 2 * core)
        self.edge, self.mid, self.inner = edge, mid, jnp.logical_not(edge | mid)
        self.core, self.inward, self.outward, self.other = core, inward, outward, other
        self.out_ref, self.own, self.pre, self.land, self.part = out_ref, own, pre, land, part

        def span(core_of, k):
            return pl.ds(pl.multiple_of(core_of * half + k * size, size), size)

        def load(k):
            return pltpu.make_async_copy(g_ref.at[:, span(core, k)], own.at[k], ld.at[k])

        def pre_copy(k):
            return remote(g_ref.at[:, span(1 - core, k)], pre.at[k], ps.at[k], pr.at[k], other)

        def in_copy(k, slot):
            return remote(part.at[k], land.at[slot, k], is_.at[k], ir.at[slot, k], inward)

        def out_copy(k):
            cut = out_ref.at[core, k]
            return remote(cut, cut, os_.at[k], or_.at[k], outward)

        def core_copy(k, which):
            cut = out_ref.at[which, k]
            return remote(cut, cut, cs.at[k], cr.at[k], other)

        self.load, self.pre_copy, self.in_copy, self.out_copy, self.core_copy = (
            load, pre_copy, in_copy, out_copy, core_copy,
        )

    def greet(self):
        signal(self.inward)
        signal(self.other)
        pl.when(jnp.logical_not(self.edge))(lambda: signal(self.outward))
        return jnp.where(self.edge, 2, 3)

    def start(self):
        for k in range(CHUNKS):
            self.pre_copy(k).start()

    def edge_in(self):
        @pl.when(self.edge)
        def _():
            for k in range(CHUNKS):
                self.load(k).wait()
                self.pre_copy(k).wait_recv()
                self.part[k] = (self.own[k].astype(f32) + self.pre[k].astype(f32)).astype(bf16)
                self.in_copy(k, 0).start()

    def pass_in(self, role, slot, k):
        @pl.when(role)
        def _():
            self.load(k).wait()
            self.pre_copy(k).wait_recv()
            total = self.own[k].astype(f32) + self.pre[k].astype(f32)
            self.in_copy(k, 0).wait_recv()
            self.part[k] = (total + self.land[0, k].astype(f32)).astype(bf16)
            self.in_copy(k, slot).start()

    def inner_in(self, k):
        self.pass_in(self.inner, 0, k)

    def mid_in(self, k):
        self.pass_in(self.mid, 1, k)

    def middle(self, k):
        @pl.when(self.mid)
        def _():
            self.in_copy(k, 1).wait_recv()
            total = self.part[k].astype(f32) + self.land[1, k].astype(f32)
            self.out_ref[pl.ds(self.core, 1), k] = total.astype(bf16)[None]
            self.out_copy(k).start()
            self.core_copy(k, self.core).start()

    def inner_out(self, k):
        @pl.when(self.inner)
        def _():
            self.out_copy(k).wait_recv()
            self.out_copy(k).start()
            self.core_copy(k, self.core).start()

    def edge_out(self, k):
        @pl.when(self.edge)
        def _():
            self.out_copy(k).wait_recv()
            self.core_copy(k, self.core).start()

    def finish(self):
        for k in range(CHUNKS):
            self.pre_copy(k).wait_send()
            self.in_copy(k, 0).wait_send()
            self.core_copy(k, self.core).wait_send()

        @pl.when(jnp.logical_not(self.edge))
        def _():
            for k in range(CHUNKS):
                self.out_copy(k).wait_send()


def adam(grad, master, moment_one, moment_two):
    one = beta_first * moment_one + (1.0 - beta_first) * grad
    two = beta_second * moment_two + (1.0 - beta_second) * grad * grad
    step_dir = one * (1.0 / bias_first) / (jnp.sqrt(two * (1.0 / bias_second)) + adam_eps)
    return one, two, master - learn_rate * step_dir


def main_kernel(
    tok_any, ids_any, gate_any, g_ref, p_ref, one_ref, two_ref, w_ref,
    newp_ref, newone_ref, newtwo_ref, out_ref,
    tok_ref, ids_ref, gate_ref, own, landing, wide_rows, gathered, w_raw, w_tmp, w_both,
    sum_ref, final, q_first, q_last, rows_first, rows_last,
    hid_own, hid_all, acc, sent, came, turned,
    ld, sems, rs, rr, ls, lr, hsems, ys, yr, cs, cr, s1, r1, s2, r2, *rest
):
    x, zh, y = place()
    w = lax.axis_index("wide")
    core = w % 2
    other = at_wide(w + 1 - 2 * core)
    expert = x * ZH + zh
    rows, columns = p_ref.shape
    half = columns // 2
    width = tok_any.shape[1]
    per = EXPERTS // 2
    batches, fit = 2, per // 2
    q_send, rows_all = (q_first, q_last), (rows_first, rows_last)
    adding = Sum(g_ref, sum_ref, *rest)

    column = [device(x, zh, (y + k) % Y) for k in range(1, Y)]
    plane = []
    for k in range(1, XZ):
        to = (expert + k) % XZ
        plane.append(device(to // ZH, to % ZH, y))
    for k in (3, 5, 1, 7, 4, 2, 6):
        signal(plane[k - 1])
    for k in (4, 3, 5, 2, 6, 1, 7):
        signal(column[k - 1])
    count = adding.greet()

    small_loads = [
        pltpu.make_async_copy(tok_any, tok_ref, ld.at[7]),
        pltpu.make_async_copy(ids_any, ids_ref, ld.at[8]),
        pltpu.make_async_copy(gate_any, gate_ref, ld.at[9]),
    ]
    for copy in small_loads:
        copy.start()
    w_load = pltpu.make_async_copy(w_ref, w_raw, ld.at[0])
    state_loads = []
    for i, which in enumerate((core, 1 - core)):
        span = pl.ds(pl.multiple_of(which * half, half), half)
        for n, (src, dst) in enumerate(
            ((p_ref, newp_ref), (one_ref, newone_ref), (two_ref, newtwo_ref))
        ):
            state_loads.append(
                pltpu.make_async_copy(src.at[:, span], dst.at[:, span], ld.at[1 + i * 3 + n])
            )
    for k in range(CHUNKS):
        adding.load(k).start()
    w_load.start()
    for copy in state_loads:
        copy.start()

    for copy in small_loads:
        copy.wait()
    own[:, :width] = tok_ref[...]
    lane = lax.broadcasted_iota(jnp.int32, (2, QBLOCK), 1)
    weights = jnp.zeros((2, QBLOCK), f32)
    for k in range(ids_ref.shape[1]):
        gate = gate_ref[:, k : k + 1].astype(f32)
        weights += jnp.where(ids_ref[:, k : k + 1] == lane, gate, 0.0)
    own[:, width:] = weights.astype(bf16)
    pl.semaphore_wait(pltpu.get_barrier_semaphore(), count + len(column) + len(plane))

    gather = Gather(own, landing, sems)
    ring = Ring(gathered, own.shape[1] // 256 * 128, rs, rr, ls, lr)
    gather.start()
    adding.start()
    adding.edge_in()

    w_load.wait()
    piece = w_tmp.shape[0]

    def split(i, carry):
        w_tmp[...] = w_raw[pl.ds(pl.multiple_of(i * piece, piece), piece), :].astype(f32)
        to = pl.ds(pl.multiple_of(i * (piece // 2), piece // 2), piece // 2)
        w_both[to, :QBLOCK] = w_tmp[pl.ds(0, piece // 2, stride=2), :].astype(bf16)
        w_both[to, QBLOCK:] = w_tmp[pl.ds(1, piece // 2, stride=2), :].astype(bf16)
        return carry

    lax.fori_loop(0, w_raw.shape[0] // piece, split, 0)

    gather.turn()
    adding.inner_in(0)
    gather.finish()
    for j in range(XZ):
        for i in range(2):
            wide_rows[i * XZ + j : i * XZ + j + 1, :] = landing[j, i : i + 1, :].astype(f32)
    gathered[pl.ds(y, 1)] = wide_rows[...].astype(bf16)[None]
    ring.start(0)
    for copy in state_loads:
        copy.wait()

    def advance(which, k, b):
        at = which * half + (k * Y + b) * QBLOCK
        cut = pl.ds(pl.multiple_of(at, QBLOCK), QBLOCK)
        one, two, updated = adam(
            sum_ref[which, k, :, b * QBLOCK : (b + 1) * QBLOCK].astype(f32),
            newp_ref[:, cut].astype(f32),
            newone_ref[:, cut],
            newtwo_ref[:, cut],
        )
        newone_ref[:, cut] = one
        newtwo_ref[:, cut] = two
        newp_ref[:, cut] = updated.astype(bf16)
        return updated

    def quantize(k):
        for b in range(Y):
            updated = advance(core, k, b)
            amax = jnp.max(jnp.abs(updated), axis=1, keepdims=True)
            scale = ((amax + amax_eps) / quant_limit).astype(bf16)
            quanta = (updated * (1.0 / scale.astype(f32))).astype(bf16)
            spot = k % fit
            q_send[k // fit][b, :, spot * QBLOCK : (spot + 1) * QBLOCK] = quanta
            q_send[1][b, :, fit * QBLOCK + k : fit * QBLOCK + k + 1] = scale

    order = [4, 3, 5, 2, 6, 1, 7]

    def relay(batch, k):
        return remote(
            q_send[batch].at[(y + k) % Y], rows_all[batch].at[core, y],
            ys.at[batch, k], yr.at[batch, k], column[k - 1],
        )

    def mine(batch):
        return pltpu.make_async_copy(
            q_send[batch].at[y], rows_all[batch].at[core, y], ys.at[batch, 0]
        )

    def relay_start(batch):
        for k in order:
            relay(batch, k).start()
        mine(batch).start()

    def share(batch, which):
        part = rows_all[batch].at[which]
        return remote(part, part, cs.at[batch], cr.at[batch], other)

    def relay_finish(batch):
        mine(batch).wait()
        for k in order:
            relay(batch, k).wait_recv()
        share(batch, core).start()

    adding.inner_in(1)
    adding.inner_in(2)
    adding.mid_in(0)
    adding.mid_in(1)
    ring.wait(0)
    ring.start(1)
    adding.inner_in(3)
    adding.mid_in(2)
    adding.middle(0)
    adding.middle(1)
    adding.mid_in(3)
    ring.wait(1)
    ring.start(2)
    adding.middle(2)
    adding.middle(3)
    adding.inner_out(0)
    adding.inner_out(1)
    ring.wait(2)
    ring.start(3)
    adding.inner_out(2)
    adding.inner_out(3)
    adding.edge_out(0)
    quantize(0)
    adding.edge_out(1)
    quantize(1)
    relay_start(0)
    ring.wait(3)

    tokens = gathered.reshape(Y * 16, own.shape[1])
    proj = jnp.dot(tokens[:, :width], w_both[...], preferred_element_type=f32)
    weight = tokens[:, width:].astype(f32)
    lanes = lax.broadcasted_iota(jnp.int32, weight.shape, 1)
    weight = jnp.sum(jnp.where(lanes == expert, weight, 0.0), axis=1, keepdims=True)
    gate = proj[:, :QBLOCK]
    hidden = weight * (gate * jax.nn.sigmoid(gate)) * proj[:, QBLOCK:]
    hid_own[...] = jnp.transpose(hidden).astype(bf16)
    hid_gather = Gather(hid_own, hid_all, hsems)
    hid_gather.start()
    adding.edge_out(2)
    quantize(2)
    adding.edge_out(3)
    quantize(3)
    relay_start(1)
    relay_finish(0)
    hid_gather.turn()
    relay_finish(1)
    hid_gather.finish()

    def products(which, j):
        total = None
        for e in range(per):
            spot = e % fit
            quanta = rows_all[e // fit][which, j, :, spot * QBLOCK : (spot + 1) * QBLOCK]
            scale = rows_all[1][which, j, :, fit * QBLOCK + e : fit * QBLOCK + e + 1].astype(f32)
            term = scale * jnp.dot(quanta, hid_all[which * per + e], preferred_element_type=f32)
            total = term if total is None else total + term
        return total

    for j in range(Y):
        acc[j, :rows] = products(core, j)
        acc[j, rows:] = jnp.zeros_like(acc[j, rows:])
    for batch in range(batches):
        share(batch, 1 - core).wait_recv()
    for j in range(Y):
        acc[j, :rows] += products(1 - core, j)

    for j in range(Y // 2):
        pair = jnp.concatenate([acc[2 * j], acc[2 * j + 1]], axis=0)
        pair = jnp.transpose(pair).astype(bf16)
        for t in range(Y):
            sent[t, :, j * QBLOCK : (j + 1) * QBLOCK] = pair[t * 16 : (t + 1) * 16]
    copies = []
    for k in order:
        to = (y + k) % Y
        copies.append(remote(sent.at[to], came.at[y], s1.at[k], r1.at[k], column[k - 1]))
        copies[-1].start()
    came[pl.ds(y, 1)] = sent[pl.ds(y, 1)]

    def other_half(k):
        adding.core_copy(k, 1 - core).wait_recv()
        for b in range(Y):
            advance(1 - core, k, b)

    other_half(0)
    other_half(1)
    for copy in copies:
        copy.wait()
    total = came[0].astype(f32)
    for j in range(1, Y):
        total += came[j].astype(f32)
    for i in range(2):
        for q in range(4):
            part = total[i * 8 : (i + 1) * 8, q * 128 : (q + 1) * 128]
            turned[:, i * 4 + q, :] = part
    copies = []
    for k in (3, 5, 1, 7, 4, 2, 6):
        to = (expert + k) % XZ
        copies.append(remote(turned.at[to], final.at[expert], s2.at[k], r2.at[k], plane[k - 1]))
        copies[-1].start()
    final[pl.ds(expert, 1)] = turned[pl.ds(expert, 1)]
    other_half(2)
    other_half(3)
    for copy in copies:
        copy.wait()
    assemble(final, out_ref, rows)

    for batch in range(batches):
        for k in order:
            relay(batch, k).wait_send()
        share(batch, core).wait_send()
    adding.finish()


def assemble(final, out_ref, rows):
    lane = lax.broadcasted_iota(jnp.int32, (2, 128), 1)
    pieces = [None] * (out_ref.shape[1] // 128)

    def add(tile, value):
        pieces[tile] = value if pieces[tile] is None else pieces[tile] + value

    for j in range(XZ):
        for q in range(4):
            pair = final[j, pl.ds(q, 2, stride=4), :]
            closed = jnp.where(lane < rows, pair, pltpu.roll(pair, 64 + rows, 1))
            closed = jnp.where(lane < 2 * rows, closed, 0.0)
            tile, shift = divmod((j * 4 + q) * 2 * rows, 128)
            turned = pltpu.roll(closed, shift, 1) if shift else closed
            add(tile, jnp.where(lane >= shift, turned, 0.0))
            if shift + 2 * rows > 128:
                add(tile + 1, jnp.where(lane < shift, turned, 0.0))
    for tile, value in enumerate(pieces):
        out_ref[:, tile * 128 : (tile + 1) * 128] = value.astype(bf16)


def store_kernel(*refs):
    sources, targets, sems = refs[:4], refs[4:8], refs[8]
    copies = [
        pltpu.make_async_copy(src, dst, sems.at[i]) for i, (src, dst) in enumerate(zip(sources, targets))
    ]
    for copy in copies:
        copy.start()
    for copy in copies:
        copy.wait()


def body(grad_parts, master, moment_one, moment_two, gate_up, tokens, expert_ids, gate_vals):
    shape = jax.ShapeDtypeStruct
    rows, columns = master.shape
    width = tokens.shape[1]
    full = width + QBLOCK
    size = columns // 2 // CHUNKS
    tok = Y * 16
    sem = DMA((CHUNKS,))
    chunk = pltpu.VMEM((CHUNKS, rows, size), bf16)
    results = pl.pallas_call(
        main_kernel,
        out_shape=(
            shape((rows, columns), bf16),
            shape((rows, columns), f32),
            shape((rows, columns), f32),
            shape((2, width), bf16),
        ),
        in_specs=[HBM] * 8,
        out_specs=(VMEM,) * 4,
        scratch_shapes=[
            pltpu.VMEM(tokens.shape, bf16),
            pltpu.VMEM(expert_ids.shape, jnp.int32),
            pltpu.VMEM(gate_vals.shape, bf16),
            pltpu.VMEM((2, full), bf16),
            pltpu.VMEM((XZ, 2, full), bf16),
            pltpu.VMEM((16, full), f32),
            pltpu.VMEM((Y, 16, full), bf16),
            pltpu.VMEM((2 * width, QBLOCK), bf16),
            pltpu.VMEM((512, QBLOCK), f32),
            pltpu.VMEM((width, 2 * QBLOCK), bf16),
            pltpu.VMEM((2, CHUNKS, rows, size), bf16),
            pltpu.VMEM((XZ, 8, 128), f32),
            pltpu.VMEM((Y, rows, 2 * QBLOCK), bf16),
            pltpu.VMEM((Y, rows, 3 * QBLOCK), bf16),
            pltpu.VMEM((2, Y, rows, 2 * QBLOCK), bf16),
            pltpu.VMEM((2, Y, rows, 3 * QBLOCK), bf16),
            pltpu.VMEM((QBLOCK, tok), bf16),
            pltpu.VMEM((XZ, QBLOCK, tok), bf16),
            pltpu.VMEM((Y, 64, tok), f32),
            pltpu.VMEM((Y, 16, 512), bf16),
            pltpu.VMEM((Y, 16, 512), bf16),
            pltpu.VMEM((XZ, 8, 128), f32),
            DMA((10,)),
        ]
        + GATHER_SEMS
        + RING_SEMS
        + GATHER_SEMS
        + [DMA((2, 8)), DMA((2, 8)), DMA((2,)), DMA((2,)), DMA((8,)), DMA((8,)), DMA((8,)), DMA((8,))]
        + [chunk, chunk, pltpu.VMEM((2, CHUNKS, rows, size), bf16), chunk]
        + [sem, sem, sem, sem, DMA((2, CHUNKS)), sem, sem, sem, sem],
        compiler_params=pltpu.CompilerParams(
            collective_id=0, has_side_effects=True, vmem_limit_bytes=36 * 2**20
        ),
    )(
        *[
            pltpu.with_memory_space_constraint(value, pltpu.HBM)
            for value in (
                tokens, expert_ids, gate_vals, grad_parts[0], master, moment_one, moment_two,
                gate_up.reshape(2 * width, QBLOCK),
            )
        ]
    )

    anywhere = pl.BlockSpec(memory_space=pl.ANY)
    return pl.pallas_call(
        store_kernel,
        out_shape=tuple(shape(value.shape, value.dtype) for value in results),
        in_specs=[VMEM] * 4,
        out_specs=(anywhere,) * 4,
        scratch_shapes=[DMA((4,))],
        compiler_params=pltpu.CompilerParams(vmem_limit_bytes=16 * 2**20),
    )(*results)


def solution(mesh):
    in_specs = (
        P("wide", "narrow", None),
        P("narrow", None),
        P("narrow", None),
        P("narrow", None),
        P(None, None, "narrow"),
        P(("wide", "narrow"), None),
        P(("wide", "narrow"), None),
        P(("wide", "narrow"), None),
    )
    out_specs = (
        P("narrow", None),
        P("narrow", None),
        P("narrow", None),
        P(("wide", "narrow"), None),
    )
    return jax.shard_map(body, mesh=mesh, in_specs=in_specs, out_specs=out_specs, check_vma=False)
```
